32 devices in a mesh: dp: 16 (over z, x, core), rep: 2 (over y).
Axes of the slice: x: 2, y: 2, z: 4, core: 2. Of those that a mesh axis runs over, the one named last changes fastest.
Arguments:
- dec_input: bfloat16 [32, 512, 768], P(('dp', 'rep')), may hold values from -6 to 6
- enc_states: bfloat16 [32, 1024, 768], P(('dp', 'rep')), may hold values from -6 to 6
- out_cotangent: bfloat16 [32, 512, 768], P(('dp', 'rep')), may hold values from -6 to 6
- dec_lengths: int32 [32], P(('dp', 'rep')), may hold values from 128 to 512, as said below
- group_ids: int32 [32], P(('dp', 'rep')), may hold values from 0 to 2
- direction_flags: int32 [32], P(('dp', 'rep')), may hold values from 0 to 1
- rel_buckets: int32 [512], replicated, may hold values from 0 to 31, as said below
- step_index: int32 [1], replicated, may hold values from 0 to 999
- self_gain: bfloat16 [768], replicated, may hold values from 0.5 to 1.5
- self_query: bfloat16 [768, 768], replicated, may hold values from -0.0390625 to 0.0390625
- self_key: bfloat16 [768, 768], replicated, may hold values from -0.21875 to 0.21875
- self_value: bfloat16 [768, 768], replicated, may hold values from -0.21875 to 0.21875
- self_output: bfloat16 [768, 768], replicated, may hold values from -0.625 to 0.625
- bucket_bias_table: bfloat16 [32, 12], replicated, may hold values from -4 to 4
- cross_gain: bfloat16 [768], replicated, may hold values from 0.5 to 1.5
- cross_query: bfloat16 [768, 768], replicated, may hold values from -0.0390625 to 0.0390625
- cross_key: bfloat16 [768, 768], replicated, may hold values from -0.21875 to 0.21875
- cross_value: bfloat16 [768, 768], replicated, may hold values from -0.21875 to 0.21875
- cross_output: bfloat16 [768, 768], replicated, may hold values from -0.625 to 0.625
- feed_gain: bfloat16 [768], replicated, may hold values from 0.5 to 1.5
- feed_inner: bfloat16 [768, 3072], replicated, may hold values from -0.21875 to 0.21875
- feed_outer: bfloat16 [3072, 768], replicated, may hold values from -0.15625 to 0.15625
- dir_table: bfloat16 [2, 768], replicated, may hold values from -3 to 3
Outputs:
- block_output: bfloat16 [32, 512, 768], P(('dp', 'rep'))
- input_grad: float32 [32, 512, 768], P(('dp', 'rep'))
- enc_grad: float32 [32, 1024, 768], P(('dp', 'rep'))
- self_gain_grad: float32 [768], P('rep')
- self_query_grad: float32 [768, 768], P('rep')
- self_key_grad: float32 [768, 768], P('rep')
- self_value_grad: float32 [768, 768], P('rep')
- self_output_grad: float32 [768, 768], P('rep')
- bias_table_grad: float32 [32, 12], P('rep')
- cross_gain_grad: float32 [768], P('rep')
- cross_query_grad: float32 [768, 768], P('rep')
- cross_key_grad: float32 [768, 768], P('rep')
- cross_value_grad: float32 [768, 768], P('rep')
- cross_output_grad: float32 [768, 768], P('rep')
- feed_gain_grad: float32 [768], P('rep')
- feed_inner_grad: float32 [768, 3072], P('rep')
- feed_outer_grad: float32 [3072, 768], P('rep')
- dir_table_grad: float32 [2, 768], P('rep')
The draws below stay inside these ranges and needn't reach their ends.
Inputs may be any that keep to these rules, and one draw needn't show every extreme that they name: `dec_lengths`: every length lies between 128 and 512; some pair has exactly 512 tokens and another exactly 128. `rel_buckets`: never falling with the distance; 0 at distance 0 and 31 at distance 512 - 1.
All inputs are finite; a program needn't handle non-finite values.
Results may differ from the reference program's by a relative error of at most 0.02.
Values sent between devices are 32-bit elements; how exact they have to be, the bound alone decides.
No kernel may reach another device: no remote copies, remote signals or barrier semaphores. Data moves between devices by JAX's collectives and lax.ppermute only.
A program may use at most 320 MiB of HBM per device.

```python
import math
import jax
import jax.numpy as jnp
from jax import lax

D = 768
H = 12
DH = 64
FF = 3072
NB = 32
DEC_LEN = 512
ENC_LEN = 1024
PERIOD = 1000
BATCH = 32


def draw_dec_lengths(key, part):
    key = jax.random.fold_in(key, 11)
    first_key, second_key, third_key = jax.random.split(key, 3)
    shortest = DEC_LEN // 4
    drawn = jax.random.randint(first_key, (BATCH,), shortest, DEC_LEN + 1)
    longest_at = jax.random.randint(second_key, (), 0, BATCH)
    shortest_at = jax.random.randint(third_key, (), 0, BATCH - 1)
    shortest_at = shortest_at + (shortest_at >= longest_at).astype(jnp.int32)
    drawn = drawn.at[longest_at].set(DEC_LEN)
    drawn = drawn.at[shortest_at].set(shortest)
    return drawn.astype(jnp.int32)


def draw_rel_buckets(key, part):
    key = jax.random.fold_in(key, 23)
    drawn = jax.random.randint(key, (DEC_LEN,), 0, NB)
    drawn = drawn.at[0].set(0)
    drawn = drawn.at[DEC_LEN - 1].set(NB - 1)
    return jnp.sort(drawn).astype(jnp.int32)


def set_ends(entries, rng, smallest, high):
    longest = entries.shape.index(max(entries.shape))
    spots = []
    for shift in (0, 1):
        where = [jax.random.randint(jax.random.fold_in(rng, axis), (), 0, length) for axis, length in enumerate(entries.shape)]
        where[longest] = (where[longest] + shift) % entries.shape[longest]
        spots.append(tuple(where))
    return entries.at[spots[0]].set(smallest).at[spots[1]].set(high)


def block_scale(own_key, dims, cuts, smallest, high):
    level, own = 1.0, jax.random.fold_in(own_key, 6)
    for position, blocks in cuts:
        heights = jnp.exp(jax.random.uniform(jax.random.fold_in(own, position), (blocks,), jnp.float32, smallest / len(cuts), high / len(cuts)))
        level = level * jnp.repeat(heights, dims[position] // blocks).reshape([-1 if axis == position else 1 for axis in range(len(dims))])
    return level


def bell_draw(own_key, extent, deviation, bound, pieces=(), kind=jnp.bfloat16):
    values = deviation * jax.random.normal(own_key, extent, jnp.float32)
    if pieces:
        values = values * block_scale(own_key, extent, pieces, -0.22, 0.18)
    return jnp.clip(values, -bound, bound).astype(kind)


def setup_inputs(seed: int = 0) -> dict:
    arg_keys = jax.random.split(jax.random.key(seed), 24)
    dec_input = bell_draw(arg_keys[0], (BATCH, DEC_LEN, D), 1.0, 6.0, ((0, 32),))
    enc_states = bell_draw(arg_keys[1], (BATCH, ENC_LEN, D), 1.0, 6.0, ((0, 32),))
    out_cotangent = bell_draw(arg_keys[2], (BATCH, DEC_LEN, D), 1.0, 6.0, ((0, 32),))
    dec_lengths = draw_dec_lengths(jax.random.fold_in(arg_keys[23], 71), 0)
    group_ids = set_ends(jax.random.randint(arg_keys[4], (BATCH,), 0, 3), jax.random.fold_in(arg_keys[4], 1), 0, 2).astype(jnp.int32)
    direction_flags = set_ends(jax.random.randint(arg_keys[5], (BATCH,), 0, 2), jax.random.fold_in(arg_keys[5], 1), 0, 1).astype(jnp.int32)
    rel_buckets = draw_rel_buckets(jax.random.fold_in(arg_keys[23], 71), 0)
    step_index = jax.random.randint(arg_keys[7], (1,), 0, PERIOD).astype(jnp.int32)
    self_gain = jnp.clip(1.0 + 0.1 * jax.random.normal(arg_keys[8], (D,), jnp.float32), 0.5, 1.5).astype(jnp.bfloat16)
    self_query = bell_draw(arg_keys[9], (D, D), (32 * D) ** -0.5, 0.0390625)
    self_key = bell_draw(arg_keys[10], (D, D), D ** -0.5, 0.21875)
    self_value = bell_draw(arg_keys[11], (D, D), D ** -0.5, 0.21875)
    self_output = bell_draw(arg_keys[12], (D, D), (D // 8) ** -0.5, 0.625)
    bucket_bias_table = bell_draw(arg_keys[13], (NB, H), 1.0, 4.0)
    cross_gain = jnp.clip(1.0 + 0.1 * jax.random.normal(arg_keys[14], (D,), jnp.float32), 0.5, 1.5).astype(jnp.bfloat16)
    cross_query = bell_draw(arg_keys[15], (D, D), (32 * D) ** -0.5, 0.0390625)
    cross_key = bell_draw(arg_keys[16], (D, D), D ** -0.5, 0.21875)
    cross_value = bell_draw(arg_keys[17], (D, D), D ** -0.5, 0.21875)
    cross_output = bell_draw(arg_keys[18], (D, D), (D // 8) ** -0.5, 0.625)
    feed_gain = jnp.clip(1.0 + 0.1 * jax.random.normal(arg_keys[19], (D,), jnp.float32), 0.5, 1.5).astype(jnp.bfloat16)
    feed_inner = bell_draw(arg_keys[20], (D, FF), D ** -0.5, 0.21875)
    feed_outer = bell_draw(arg_keys[21], (FF, D), (FF // 2) ** -0.5, 0.15625)
    dir_table = bell_draw(arg_keys[22], (2, D), 0.5, 3.0)
    return dict(dec_input=dec_input, enc_states=enc_states, out_cotangent=out_cotangent, dec_lengths=dec_lengths, group_ids=group_ids, direction_flags=direction_flags, rel_buckets=rel_buckets, step_index=step_index, self_gain=self_gain, self_query=self_query, self_key=self_key, self_value=self_value, self_output=self_output, bucket_bias_table=bucket_bias_table, cross_gain=cross_gain, cross_query=cross_query, cross_key=cross_key, cross_value=cross_value, cross_output=cross_output, feed_gain=feed_gain, feed_inner=feed_inner, feed_outer=feed_outer, dir_table=dir_table)


highest_precision = lax.Precision.HIGHEST
full_turn = 2.0 * math.pi
norm_eps = 1e-06
masked_score = -1e+30

@jax.custom_vjp
def low(v):
    return lax.optimization_barrier(v.astype(jnp.bfloat16)).astype(jnp.float32)

@jax.custom_vjp
def low_back(v):
    return v

def low_keep(v):
    return (low(v), None)

def low_pass(kept, grad):
    return (grad,)

def back_keep(v):
    return (v, None)

def back_low(kept, grad):
    return (low(grad),)
low.defvjp(low_keep, low_pass)
low_back.defvjp(back_keep, back_low)

def matmul(left_side, right_side):
    return jnp.dot(left_side, right_side, precision=highest_precision, preferred_element_type=jnp.float32)

def rms_norm(inputs, gain):
    return inputs * lax.rsqrt(lax.optimization_barrier(jnp.mean(inputs * inputs, axis=-1, keepdims=True)) + norm_eps) * gain

def attend(queries, key_rows, value_rows, extra, allowed):
    query_heads = queries.reshape(queries.shape[0], H, DH)
    key_heads = key_rows.reshape(key_rows.shape[0], H, DH)
    value_heads = value_rows.reshape(value_rows.shape[0], H, DH)
    raw_scores = low_back(jnp.einsum('qhd,khd->hqk', query_heads, key_heads, precision=highest_precision))
    scores = raw_scores + extra
    if allowed is not None:
        scores = jnp.where(allowed[None], scores, masked_score)
    prob_rows = low(jax.nn.softmax(scores, axis=-1))
    mixed = jnp.einsum('hqk,khd->qhd', prob_rows, value_heads, precision=highest_precision)
    return low(low_back(mixed.reshape(queries.shape[0], D)))

def forward(params, dec_rows, enc_rows, flag_value, valid_rows, bucket_onehot, causal):
    gain_a, query_w, key_w, value_w, output_w, table_weight, gain_b, cross_qw, cross_kw, cross_vw, cross_ow, gain_c, inner_w, outer_w, dir_w = params
    position_bias = jnp.einsum('fjx,fv->vjx', bucket_onehot, table_weight, precision=highest_precision)
    stream0 = dec_rows + jnp.where(flag_value == 0, dir_w[0], dir_w[1])
    input_a = low(rms_norm(stream0, gain_a))
    queries = low(low_back(matmul(input_a, query_w)))
    key_rows = low(low_back(matmul(input_a, key_w)))
    value_rows = low(low_back(matmul(input_a, value_w)))
    stream1 = stream0 + low_back(matmul(attend(queries, key_rows, value_rows, position_bias, causal), output_w))
    input_b = low(rms_norm(stream1, gain_b))
    cross_q = low(low_back(matmul(input_b, cross_qw)))
    enc_keys = low(low_back(matmul(enc_rows, cross_kw)))
    enc_values = low(low_back(matmul(enc_rows, cross_vw)))
    stream2 = stream1 + low_back(matmul(attend(cross_q, enc_keys, enc_values, 0.0, None), cross_ow))
    input_c = low(rms_norm(stream2, gain_c))
    inner_act = low_back(matmul(input_c, inner_w))
    active = low(jax.nn.gelu(inner_act, approximate=True))
    return valid_rows * (stream2 + low_back(matmul(active, outer_w)))

def reference(dec_input, enc_states, out_cotangent, dec_lengths, group_ids, direction_flags, rel_buckets, step_index, self_gain, self_query, self_key, self_value, self_output, bucket_bias_table, cross_gain, cross_query, cross_key, cross_value, cross_output, feed_gain, feed_inner, feed_outer, dir_table):
    params = tuple((item.astype(jnp.float32) for item in (self_gain, self_query, self_key, self_value, self_output, bucket_bias_table, cross_gain, cross_query, cross_key, cross_value, cross_output, feed_gain, feed_inner, feed_outer, dir_table)))
    row_pos = lax.broadcasted_iota(jnp.int32, (DEC_LEN, DEC_LEN), 0)
    col_pos = lax.broadcasted_iota(jnp.int32, (DEC_LEN, DEC_LEN), 1)
    causal = col_pos <= row_pos
    bucket_map = jnp.take(rel_buckets, jnp.maximum(row_pos - col_pos, 0).astype(jnp.int32))
    bucket_ids = lax.broadcasted_iota(jnp.int32, (NB, 1, 1), 0)
    bucket_onehot = jnp.where((bucket_map[None] == bucket_ids) & causal[None], 1.0, 0.0).astype(jnp.float32)
    phase = full_turn * step_index[0].astype(jnp.float32) / PERIOD

    def per_pair(totals, entry):
        dec_rows, enc_rows, cot_rows, length, group_id, flag_value = entry
        valid_rows = (lax.iota(jnp.int32, DEC_LEN) < length).astype(jnp.float32)[:, None]
        weight = 1.0 + 0.5 * jnp.cos(phase + full_turn * group_id.astype(jnp.float32) / 3.0)

        def local_block(param_set, dec_part, enc_part):
            return forward(param_set, dec_part, enc_part, flag_value, valid_rows, bucket_onehot, causal)
        result, pull_back = jax.vjp(local_block, params, dec_rows.astype(jnp.float32), enc_rows.astype(jnp.float32))
        param_grads, dec_grad, enc_grad = pull_back(cot_rows.astype(jnp.float32) * weight)
        totals = jax.tree.map(jnp.add, totals, param_grads)
        return (totals, (result.astype(jnp.bfloat16), dec_grad, enc_grad))
    start = tuple((jnp.zeros(item.shape, jnp.float32) for item in params))
    totals, (outputs, dec_grads, enc_grads) = lax.scan(per_pair, start, (dec_input, enc_states, out_cotangent, dec_lengths, group_ids, direction_flags))
    return (outputs, dec_grads, enc_grads, totals[0], totals[1], totals[2], totals[3], totals[4], totals[5], totals[6], totals[7], totals[8], totals[9], totals[10], totals[11], totals[12], totals[13], totals[14])
```

```python
from functools import partial
import math

import jax
import jax.numpy as jnp
from jax import lax
from jax.experimental import pallas as pl
from jax.experimental.pallas import tpu as pltpu
from jax.sharding import PartitionSpec as P

PERIOD = 1000
full_turn = 2.0 * math.pi
norm_eps = 1e-06
masked_score = -1e30
LANES = 128
FLOPS = 2 * 10**10
BYTES = 10**7
f32 = jnp.float32
bf16 = jnp.bfloat16

NN = (((1,), (0,)), ((), ()))
NT = (((1,), (1,)), ((), ()))
TN = (((0,), (0,)), ((), ()))


def dot(left, right, form):
    return lax.dot_general(left, right, form, preferred_element_type=f32)


def shaped(shape, dtype):
    return jax.ShapeDtypeStruct(shape, dtype)


class Order:
    def __init__(self):
        self.last, self.held = None, False

    def call(self, kernel, *, in_specs, out_shape, out_specs, vmem, **more):
        count = len(in_specs)
        held = lambda shape, spec: pltpu.HBM(shape.shape, shape.dtype) if spec is HBM else shape
        if isinstance(out_specs, list):
            out_shape = [held(a, b) for a, b in zip(out_shape, out_specs)]
        else:
            out_shape = held(out_shape, out_specs)

        def apply(*args):
            after = [] if self.last is None or any(self.last is a for a in args) else [self.last]
            if self.held:
                after = [pltpu.with_memory_space_constraint(a, pltpu.HBM) for a in after]

            def ordered(*refs):
                return kernel(*refs[:count], *refs[count + len(after) :])

            args = [
                pltpu.with_memory_space_constraint(a, pltpu.HBM) if s is HBM or s is FROM_HBM else a
                for a, s in zip(args, in_specs)
            ]
            outs = pl.pallas_call(
                ordered,
                in_specs=list(in_specs) + [ANY] * len(after),
                out_shape=out_shape,
                out_specs=out_specs,
                compiler_params=pltpu.CompilerParams(vmem_limit_bytes=vmem * 2**20),
                cost_estimate=pl.CostEstimate(flops=FLOPS, bytes_accessed=BYTES, transcendentals=0),
                **more,
            )(*args, *after)
            self.last, self.held = jax.tree.leaves(outs)[0], jax.tree.leaves(out_specs)[0] is HBM
            return outs

        return apply


HBM = pl.BlockSpec(memory_space=pltpu.HBM)
ANY = pl.BlockSpec(memory_space=pl.ANY)
VM = pl.BlockSpec(memory_space=pltpu.VMEM)
FROM_HBM = pl.BlockSpec(memory_space=pltpu.VMEM)
SM = pl.BlockSpec(memory_space=pltpu.SMEM)
AXES = {"y": 1, "z": 2, "x": 3}


class Moves:
    def __init__(self, sems):
        self.sems, self.count, self.stores = sems, 0, []

    def load(self, source, target):
        copy = pltpu.make_async_copy(source, target, self.sems.at[self.count])
        self.count += 1
        copy.start()
        return copy

    def store(self, source, target):
        self.stores.append(self.load(source, target))

    def finish(self):
        for copy in self.stores:
            copy.wait()


def norm_rows(stream, gain):
    scale = lax.rsqrt(jnp.mean(stream * stream, axis=-1, keepdims=True) + norm_eps)
    return stream * scale * gain


def norm_pull(grad_out, stream, gain):
    scale = lax.rsqrt(jnp.mean(stream * stream, axis=-1, keepdims=True) + norm_eps)
    normed = stream * scale
    gain_grad = jnp.sum(grad_out * normed, axis=0, keepdims=True)
    grad_normed = grad_out * gain
    inner_mean = jnp.mean(grad_normed * normed, axis=-1, keepdims=True)
    return scale * (grad_normed - normed * inner_mean), gain_grad


def weighted(cot, length, weight):
    valid = (lax.broadcasted_iota(jnp.int32, (cot.shape[0], 1), 0) < length[0]).astype(f32)
    return valid, valid * (cot[...].astype(f32) * weight[0])


def head_masks(width, head_size):
    lane = lax.broadcasted_iota(jnp.int32, (1, width), 1)
    return [jnp.where(lane // head_size == i, 1.0, 0.0).astype(f32) for i in range(width // head_size)]


def pair_lanes(index):
    return pl.ds(pl.multiple_of(index * LANES, LANES), LANES)


def half_lanes(half, width):
    return pl.ds(pl.multiple_of(half * (width // 2), LANES), width // 2)


def forward_kernel(
    head_size, num_buckets,
    flag, self_gain, cross_gain, feed_gain, dirs, buckets, table, dec, enc, wq, wk, wv, wo, cq, ck, cv, co,
    o_input_a, o_q, o_k, o_v, o_mixed_a, o_stream1, o_input_b, o_cq, o_ek, o_ev, o_mixed_b, o_stream2, o_input_c,
    o_pa, o_pb, rows, o_inv_a, o_inv_b,
    v_dec, v_enc, v_wq, v_wk, v_wv, v_wo, v_cq, v_ck, v_cv, v_co,
    input_a, q, k, v, mixed_a, stream1, input_b, xq, ek, ev, mixed_b, stream2, input_c,
    dist, slots_a, slots_b, sems, slot_sems,
):
    dec_len, width = dec.shape
    pairs = width // LANES
    per = LANES // head_size
    moves = Moves(sems)
    names = (v_dec, v_wq, v_wk, v_wv, v_enc, v_ck, v_cv, v_wo, v_cq, v_co)
    loads = [moves.load(s, t) for s, t in zip((dec, wq, wk, wv, enc, ck, cv, wo, cq, co), names)]
    flat = lambda ref: ref[...].astype(f32).reshape(1, ref.shape[0])
    gain_a, gain_b, gain_c = flat(self_gain), flat(cross_gain), flat(feed_gain)
    rows[...] = jnp.zeros(rows.shape, f32)
    for i, row in enumerate((gain_a, gain_b, gain_c)):
        rows[i : i + 1, :] = row
    rows[3:5, :] = dirs[...].astype(f32)
    rows[5:6, 0:dec_len] = flat(buckets)
    pick = lax.broadcasted_iota(jnp.int32, (num_buckets, dec_len), 0).astype(f32) == rows[5:6, :dec_len]
    dist[0 : table.shape[0], :] = dot(table[...], jnp.where(pick, 1.0, 0.0).astype(bf16), NN)
    dir_row = jnp.where(flag[0] == 0, rows[3:4, :], rows[4:5, :])
    loads[0].wait()
    input_a[...] = norm_rows(v_dec[...].astype(f32) + dir_row, gain_a).astype(bf16)
    moves.store(input_a, o_input_a)
    for load, weight, target, out in ((1, v_wq, q, o_q), (2, v_wk, k, o_k), (3, v_wv, v, o_v)):
        loads[load].wait()
        target[...] = dot(input_a[...], weight[...], NN).astype(bf16)
        moves.store(target, out)
    loads[4].wait()
    for load, weight, target, out in ((5, v_ck, ek, o_ek), (6, v_cv, ev, o_ev)):
        loads[load].wait()
        target[...] = dot(v_enc[...], weight[...], NN).astype(bf16)
        moves.store(target, out)
    masks = head_masks(LANES, head_size)
    edge = dec_len // 2
    key_pos = lax.broadcasted_iota(jnp.int32, (edge, edge), 0)
    query_pos = lax.broadcasted_iota(jnp.int32, (edge, edge), 1)

    def attend(queries, keys, values, mixed, slots, out, inverse, head_rows):
        def slot_copy(index, slot):
            return pltpu.make_async_copy(slots.at[slot], out.at[pl.ds(index * per, per)], slot_sems.at[slot])

        def body(index, carry):
            slot = lax.rem(index, 2)

            @pl.when(index >= 2)
            def _():
                slot_copy(index - 2, slot).wait()

            lanes = pair_lanes(index)
            key_block, value_rows, query_block = keys[:, lanes], values[:, lanes].T, queries[:, lanes]
            ones = jnp.ones((16, value_rows.shape[1]), bf16)
            parts, sums = [], []
            for i in range(per):
                mix = jnp.concatenate([value_rows[i * head_size : (i + 1) * head_size], ones], axis=0)
                total = head_rows(index, i, slot, key_block, query_block * masks[i].astype(bf16), mix)
                inv = 1.0 / total[head_size : head_size + 1, :]
                parts.append(total[0:head_size, :] * inv)
                sums.append(inv)
            mixed[:, lanes] = jnp.concatenate(parts, axis=0).T.astype(bf16)
            inverse[pl.ds(index, 1)] = jnp.concatenate(sums, axis=0)[None]
            slot_copy(index, slot).start()
            return carry

        lax.fori_loop(0, pairs, body, 0)
        for index in range(max(pairs - 2, 0), pairs):
            slot_copy(index, index % 2).wait()

    def raised(scores, top):
        return jnp.exp(scores - top).astype(bf16)

    def own_rows(index, i, slot, key_block, query, mix):
        row = dist[pl.ds(index * per + i, 1), :]
        bias = pltpu.roll(jnp.broadcast_to(row, (edge, dec_len)), 0, 1, stride=1, stride_axis=0)
        seen = key_pos <= query_pos
        low, high = slice(0, edge), slice(edge, dec_len)
        near = jnp.where(seen, dot(key_block[low], query[low], NT) + bias[:, low], masked_score)
        first = raised(near, jnp.max(near, axis=0, keepdims=True))
        slots_a[slot, i, low, low] = first
        far = dot(key_block[low], query[high], NT) + bias[:, high]
        near = jnp.where(seen, dot(key_block[high], query[high], NT) + bias[:, low], masked_score)
        top = jnp.maximum(jnp.max(far, axis=0, keepdims=True), jnp.max(near, axis=0, keepdims=True))
        second, third = raised(far, top), raised(near, top)
        slots_a[slot, i, low, high] = second
        slots_a[slot, i, high, high] = third
        right = dot(mix[:, low], second, NN) + dot(mix[:, high], third, NN)
        return jnp.concatenate([dot(mix[:, low], first, NN), right], axis=1)

    def cross_rows(index, i, slot, key_block, query, mix):
        scores = dot(key_block, query, NT)
        low = raised(scores, jnp.max(scores, axis=0, keepdims=True))
        slots_b[slot, i] = low
        return dot(mix, low, NN)

    attend(q, k, v, mixed_a, slots_a, o_pa, o_inv_a, own_rows)
    moves.store(mixed_a, o_mixed_a)
    loads[7].wait()
    stream1[...] = v_dec[...].astype(f32) + dir_row + dot(mixed_a[...], v_wo[...], NN)
    moves.store(stream1, o_stream1)
    input_b[...] = norm_rows(stream1[...], gain_b).astype(bf16)
    moves.store(input_b, o_input_b)
    loads[8].wait()
    xq[...] = dot(input_b[...], v_cq[...], NN).astype(bf16)
    moves.store(xq, o_cq)
    attend(xq, ek, ev, mixed_b, slots_b, o_pb, o_inv_b, cross_rows)
    moves.store(mixed_b, o_mixed_b)
    loads[9].wait()
    stream2[...] = stream1[...] + dot(mixed_b[...], v_co[...], NN)
    moves.store(stream2, o_stream2)
    input_c[...] = norm_rows(stream2[...], gain_c).astype(bf16)
    moves.store(input_c, o_input_c)
    moves.finish()


def forward(order, head_size, num_buckets, flag, smalls, dec, enc, weights):
    t, d = dec.shape
    e = enc.shape[0]
    heads = d // head_size
    per = LANES // head_size
    td, ed = (t, d), (e, d)
    low = [td, td, td, td, td, None, td, td, ed, ed, td, None, td]
    outs = [shaped(s, bf16) if s else shaped(td, f32) for s in low]
    outs += [shaped((heads, t, t), bf16), shaped((heads, e, t), bf16), shaped((8, d), f32)]
    outs += [shaped((heads // per, per, t), f32)] * 2
    scratch = [pltpu.VMEM(td, bf16), pltpu.VMEM(ed, bf16)] + [pltpu.VMEM((d, d), bf16)] * 8
    scratch += [pltpu.VMEM(s, bf16) if s else pltpu.VMEM(td, f32) for s in low]
    scratch += [
        pltpu.VMEM((-(-heads // 8) * 8, t), f32),
        pltpu.VMEM((2, per, t, t), bf16),
        pltpu.VMEM((2, per, e, t), bf16),
        pltpu.SemaphoreType.DMA((23,)),
        pltpu.SemaphoreType.DMA((2,)),
    ]
    return order.call(
        partial(forward_kernel, head_size, num_buckets),
        out_shape=outs,
        in_specs=[SM] + [FROM_HBM] * 6 + [HBM] * 10,
        out_specs=[HBM] * (len(outs) - 3) + [VM] * 3,
        scratch_shapes=scratch,
        vmem=48,
        name="forward",
    )(flag, *smalls, dec, enc, *weights)


def feed_kernel(
    offset, place, weight, length, cot, input_c, w1, w2, o_active, o_pull, o_sent,
    v_cot, v_input, v_w1, v_w2, grad_low, active, pull, sent, sems,
):
    d = cot.shape[1]
    split = v_w1.shape[2]
    block = w1.shape[1] // 2
    rows = d // 2
    moves = Moves(sems)
    columns = [pl.ds(b * block + offset, split) for b in range(2)]
    got_input = moves.load(input_c, v_input)
    got = [[moves.load(w1.at[:, columns[0]], v_w1.at[0])], []]
    got_cot = moves.load(cot, v_cot)
    got[0].append(moves.load(w2.at[columns[0], :], v_w2.at[0]))
    got[1] += [moves.load(w1.at[:, columns[1]], v_w1.at[1]), moves.load(w2.at[columns[1], :], v_w2.at[1])]
    other = 1 - place[0]
    lanes = half_lanes(other, d)
    got_input.wait()
    for b in range(2):
        got[b][0].wait()
        inner = dot(v_input[...], v_w1[b], NN)
        if b == 0:
            got_cot.wait()
            grad_low[...] = weighted(v_cot, length, weight)[1].astype(bf16)
        got[b][1].wait()
        back = dot(grad_low[...], v_w2[b], NT)
        root = math.sqrt(2.0 / math.pi)
        square = inner * inner
        bent = jnp.tanh(root * (inner + 0.044715 * (square * inner)))
        half_up = 0.5 * (1.0 + bent)
        slope = half_up + (0.5 * inner) * (1.0 - bent * bent) * (root * (1.0 + 3.0 * 0.044715 * square))
        active[b] = (inner * half_up).astype(bf16)
        moves.store(active.at[b], o_active.at[b])
        pull[b] = (back * slope).astype(bf16)
        moves.store(pull.at[b], o_pull.at[b])
    for b in range(2):
        sent[b, 0:split, :] = dot(active[b], grad_low[:, lanes], TN)
        for i in range(split // rows):
            sent[b, split + i * rows : split + (i + 1) * rows, :] = dot(
                v_input[:, b * rows : (b + 1) * rows], pull[other, :, i * rows : (i + 1) * rows], TN
            )
        moves.store(sent.at[b], o_sent.at[b])
    moves.finish()


def feed(order, offset, split, place, weight, length, cot, input_c, w1, w2):
    t, d = cot.shape
    wide = (2, t, split)
    out = (2, 2 * split, d // 2)
    return order.call(
        partial(feed_kernel, offset),
        out_shape=[shaped(wide, bf16), shaped(wide, bf16), shaped(out, f32)],
        in_specs=[SM, SM, SM, HBM, HBM, HBM, HBM],
        out_specs=[HBM] * 3,
        scratch_shapes=[
            pltpu.VMEM((t, d), bf16),
            pltpu.VMEM((t, d), bf16),
            pltpu.VMEM((2, d, split), bf16),
            pltpu.VMEM((2, split, d), bf16),
            pltpu.VMEM((t, d), bf16),
            pltpu.VMEM(wide, bf16),
            pltpu.VMEM(wide, bf16),
            pltpu.VMEM(out, f32),
            pltpu.SemaphoreType.DMA((12,)),
        ],
        vmem=32,
        name="feed",
    )(place, weight, length, cot, input_c, w1, w2)


def bit_of(place, axes):
    return jnp.where(place[0] == 0, place[AXES[axes[0]]], place[AXES[axes[1]]])


def cut_first(axes, place, full, out_send, out_keep):
    count = full.shape[1] // 2
    for core in range(2):

        @pl.when(place[0] == core)
        def _(core=core):
            bit = place[AXES[axes[core]]]
            for out, at in ((out_send, 1 - bit), (out_keep, bit)):
                if axes[core] == "y":
                    out[...] = full[at]
                else:
                    for b in range(2):
                        out[b * count : (b + 1) * count, :] = full[b, pl.ds(pl.multiple_of(at * count, 8), count), :]


def feed_kept_kernel(
    axes, place, weight, length, cot, input_c, active, pull, sent, o_send, o_keep,
    v_cot, v_input, v_active, v_pull, v_sent, grad_low, full, sems,
):
    d = cot.shape[1]
    split = active.shape[2]
    rows = d // 2
    half = place[0]
    moves = Moves(sems)
    lanes = half_lanes(half, d)
    got = [moves.load(cot.at[:, lanes], v_cot), moves.load(active, v_active), moves.load(sent, v_sent)]
    got += [moves.load(input_c, v_input), moves.load(pull.at[half], v_pull)]
    got[0].wait()
    grad_low[...] = weighted(v_cot, length, weight)[1].astype(bf16)
    got[1].wait()
    got[2].wait()
    for b in range(2):
        full[b, 0:split, :] = v_sent[b, 0:split, :] + dot(v_active[b], grad_low[...], TN)
    got[3].wait()
    got[4].wait()
    for b in range(2):
        for i in range(split // rows):
            here = slice(split + i * rows, split + (i + 1) * rows)
            full[b, here, :] = v_sent[b, here, :] + dot(
                v_input[:, b * rows : (b + 1) * rows], v_pull[:, i * rows : (i + 1) * rows], TN
            )
    cut_first(axes, place, full, o_send, o_keep)


def feed_kept(order, axes, place, weight, length, cot, input_c, active, pull, sent):
    t, d = cot.shape
    split = active.shape[2]
    return order.call(
        partial(feed_kept_kernel, axes),
        out_shape=[shaped(sent.shape[1:], f32)] * 2,
        in_specs=[SM, SM, SM] + [HBM] * 4 + [ANY],
        out_specs=[VM] * 2,
        scratch_shapes=[
            pltpu.VMEM((t, d // 2), bf16),
            pltpu.VMEM((t, d), bf16),
            pltpu.VMEM((2, t, split), bf16),
            pltpu.VMEM((t, split), bf16),
            pltpu.VMEM(sent.shape, f32),
            pltpu.VMEM((t, d // 2), bf16),
            pltpu.VMEM(sent.shape, f32),
            pltpu.SemaphoreType.DMA((5,)),
        ],
        vmem=30,
        name="feed_kept",
    )(place, weight, length, cot, input_c, active, pull, sent)


def close_kernel(cuts, *refs):
    parts = len(cuts)
    weight, length, rows, cot, stream2 = refs[:5]
    pulls = refs[5 : 5 + parts]
    w1, wo, o_grad, o_low, o_mixed, o_gain, v_cot, v_stream, v_pull, v_w1, v_wo, grad, low, mixed, sems = refs[5 + parts :]
    block = w1.shape[1] // 2
    moves = Moves(sems)
    got = []
    for b in range(2):
        for p, (offset, split) in enumerate(cuts):
            here = pl.ds(b * block + offset, split)
            got.append(moves.load(pulls[p].at[b], v_pull.at[:, here]))
            got.append(moves.load(w1.at[:, here], v_w1.at[:, here]))
    got_stream, got_cot = moves.load(stream2, v_stream), moves.load(cot, v_cot)
    got_wo = moves.load(wo, v_wo)
    back = None
    for b in range(2):
        here = slice(b * block, (b + 1) * block)
        for copy in got[b * 2 * parts : (b + 1) * 2 * parts]:
            copy.wait()
        term = dot(v_pull[:, here], v_w1[:, here], NT)
        back = term if back is None else back + term
    got_stream.wait()
    pulled, gain_grad = norm_pull(back, v_stream[...], rows[2:3, :])
    o_gain[...] = gain_grad
    got_cot.wait()
    grad[...] = pulled + weighted(v_cot, length, weight)[1]
    moves.store(grad, o_grad)
    low[...] = grad[...].astype(bf16)
    moves.store(low, o_low)
    got_wo.wait()
    mixed[...] = dot(low[...], v_wo[...], NT).astype(bf16)
    moves.store(mixed, o_mixed)
    moves.finish()


def close(order, cuts, weight, length, rows, cot, stream2, pulls, w1, wo):
    t, d = cot.shape
    parts = len(cuts)
    td = (t, d)
    return order.call(
        partial(close_kernel, cuts),
        out_shape=[shaped(td, f32), shaped(td, bf16), shaped(td, bf16), shaped((1, d), f32)],
        in_specs=[SM, SM, VM] + [HBM] * (4 + parts),
        out_specs=[HBM] * 3 + [VM],
        scratch_shapes=[
            pltpu.VMEM(td, bf16),
            pltpu.VMEM(td, f32),
            pltpu.VMEM((t, w1.shape[1]), bf16),
            pltpu.VMEM(w1.shape, bf16),
            pltpu.VMEM((d, d), bf16),
            pltpu.VMEM(td, f32),
            pltpu.VMEM(td, bf16),
            pltpu.VMEM(td, bf16),
            pltpu.SemaphoreType.DMA((4 * parts + 6,)),
        ],
        vmem=30,
        name="close",
    )(weight, length, rows, cot, stream2, *pulls, w1, wo)


def result_kernel(cuts, *refs):
    parts = len(cuts)
    length, stream2 = refs[:2]
    actives = refs[2 : 2 + parts]
    w2, out, v_stream, v_active, v_w2, sems = refs[2 + parts :]
    block = w2.shape[0] // 2
    moves = Moves(sems)
    got = []
    for b in range(2):
        for p, (offset, split) in enumerate(cuts):
            here = pl.ds(b * block + offset, split)
            got.append(moves.load(actives[p].at[b], v_active.at[:, here]))
            got.append(moves.load(w2.at[here, :], v_w2.at[here, :]))
    got.append(moves.load(stream2, v_stream))
    for copy in got:
        copy.wait()
    valid = (lax.broadcasted_iota(jnp.int32, (out.shape[0], 1), 0) < length[0]).astype(f32)
    out[...] = (valid * (v_stream[...] + dot(v_active[...], v_w2[...], NN))).astype(bf16)


def block_result(order, cuts, length, stream2, actives, w2):
    t, d = stream2.shape
    parts = len(cuts)
    return order.call(
        partial(result_kernel, cuts),
        out_shape=shaped((t, d), bf16),
        in_specs=[SM] + [HBM] * (2 + parts),
        out_specs=VM,
        scratch_shapes=[
            pltpu.VMEM((t, d), f32),
            pltpu.VMEM((t, w2.shape[0]), bf16),
            pltpu.VMEM(w2.shape, bf16),
            pltpu.SemaphoreType.DMA((4 * parts + 1,)),
        ],
        vmem=24,
        name="result",
    )(length, stream2, *actives, w2)


def fold_diagonals(tiles):
    count, length = tiles.shape
    steps = LANES // 8
    total = None
    for u in range(steps):
        acc = None
        for k in range(count // LANES):
            t = k * steps + u
            tile = tiles[8 * t : 8 * t + 8, :]
            if k:
                tile = jnp.concatenate([tile[:, LANES * k :], tile[:, : LANES * k]], axis=1)
            acc = tile if acc is None else acc + tile
        if u:
            acc = pltpu.roll(acc, length - 8 * u, 1)
        total = acc if total is None else total + acc
    rows = lax.broadcasted_iota(jnp.int32, (8, length), 0)
    for b in (1, 2, 4):
        total = jnp.where((rows & b) != 0, pltpu.roll(total, length - b, 1), total)
    return total


def attend_back_kernel(head_size, fold, first, count, earlier, inverse, probs, grad_mixed, queries, keys, values, *refs):
    refs = refs[earlier:]
    o_q, o_k, o_v = refs[:3]
    o_dist = refs[3] if fold else None
    v_grad, v_q, v_k, v_v, v_dq, v_dk, v_dv, slots, sems, slot_sems = refs[3 + fold : 13 + fold]
    v_dist = refs[13 + fold] if fold else None
    per = LANES // head_size
    masks = head_masks(LANES, head_size)

    def there(index):
        return pl.ds(pl.multiple_of((first + index) * LANES, LANES), LANES)

    def pair_loads(index):
        both = zip((values, grad_mixed, keys, queries), (v_v, v_grad, v_k, v_q))
        return [
            pltpu.make_async_copy(s.at[:, there(index)], t.at[:, pair_lanes(index)], sems.at[index, i])
            for i, (s, t) in enumerate(both)
        ]

    def pair_stores(index):
        both = zip((v_dq, v_dk, v_dv), (o_q, o_k, o_v))
        return [
            pltpu.make_async_copy(s.at[:, pair_lanes(index)], t.at[:, there(index)], sems.at[index, 4 + i])
            for i, (s, t) in enumerate(both)
        ]

    def slot_copy(index):
        slot = lax.rem(index, 2)
        return pltpu.make_async_copy(probs.at[pl.ds((first + index) * per, per)], slots.at[slot], slot_sems.at[slot])

    for copy in pair_loads(0):
        copy.start()
    slot_copy(0).start()
    for index in range(1, count):
        for copy in pair_loads(index):
            copy.start()

    def block(low, value, grad, inv):
        full = low.astype(f32)
        prob_grad = dot(value, grad, NT)
        return full, prob_grad, jnp.sum(full * prob_grad, axis=0, keepdims=True)

    def body(index, carry):
        @pl.when(index + 1 < count)
        def _():
            slot_copy(index + 1).start()

        lanes = pair_lanes(index)
        slot = lax.rem(index, 2)
        for copy in pair_loads(index):
            copy.wait()
        key_block, value_block, query_block, grad_block = v_k[:, lanes], v_v[:, lanes], v_q[:, lanes], v_grad[:, lanes]
        inv_rows = inverse[pl.ds(first + index, 1)][0]
        inv_columns = jnp.concatenate([inv_rows, jnp.zeros((8 - per, inv_rows.shape[1]), f32)], axis=0).T
        scaled = grad_block.astype(f32) * sum(inv_columns[:, i : i + 1] * masks[i] for i in range(per))
        scaled = scaled.astype(bf16)
        slot_copy(index).wait()
        grads = [0.0, 0.0, 0.0]
        for i in range(per):
            inv = inv_rows[i : i + 1, :]
            grad = scaled * masks[i].astype(bf16)
            if fold:
                edge = grad.shape[0] // 2
                low, high = slice(0, edge), slice(edge, 2 * edge)
                cuts = ((low, low), (low, high), (high, high))
                probs_at = [slots[slot, i, k, q] for k, q in cuts]
                full, back, sums = zip(*(block(p, value_block[k], grad[q], inv) for p, (k, q) in zip(probs_at, cuts)))
                sums = (sums[0], sums[1] + sums[2], sums[1] + sums[2])
                scores = [f * (g - s * inv[:, q]) for f, g, s, (k, q) in zip(full, back, sums, cuts)]
                v_dist[index * per + i] = fold_diagonals(jnp.concatenate([scores[0] + scores[2], scores[1]], axis=1))
                lows = [x.astype(bf16) for x in scores]
                dq = [dot(lows[0], key_block[low], TN), dot(lows[1], key_block[low], TN) + dot(lows[2], key_block[high], TN)]
                dk = [dot(lows[0], query_block[low], NN) + dot(lows[1], query_block[high], NN), dot(lows[2], query_block[high], NN)]
                dv = [dot(probs_at[0], scaled[low], NN) + dot(probs_at[1], scaled[high], NN), dot(probs_at[2], scaled[high], NN)]
                terms_of = [jnp.concatenate(x, axis=0) for x in (dq, dk, dv)]
            else:
                probs_all = slots[slot, i]
                full, back, total = block(probs_all, value_block, grad, inv)
                score_low = (full * (back - total * inv)).astype(bf16)
                terms_of = [dot(score_low, key_block, TN), dot(score_low, query_block, NN), dot(probs_all, scaled, NN)]
            grads = [g + x * masks[i] for g, x in zip(grads, terms_of)]
        v_dq[:, lanes] = grads[0].astype(bf16)
        v_dk[:, lanes] = grads[1].astype(bf16)
        v_dv[:, lanes] = grads[2].astype(bf16)
        for copy in pair_stores(index):
            copy.start()
        return carry

    lax.fori_loop(0, count, body, 0)
    if fold:
        dist_copy = pltpu.make_async_copy(v_dist, o_dist.at[pl.ds(first * per, count * per)], sems.at[0, 7])
        dist_copy.start()
        dist_copy.wait()
    for index in range(count):
        for copy in pair_stores(index):
            copy.wait()


def attend_back(order, head_size, fold, first, count, inverse, probs, grad_mixed, queries, keys, values, earlier=()):
    t, d = queries.shape
    e = keys.shape[0]
    per = LANES // head_size
    td, ed = (t, count * LANES), (e, count * LANES)
    out_shape = [shaped((t, d), bf16), shaped((e, d), bf16), shaped((e, d), bf16)]
    if fold:
        out_shape.append(shaped((d // head_size, 8, t), f32))
    scratch = [pltpu.VMEM(s, bf16) for s in (td, td, ed, ed, td, ed, ed)]
    scratch += [pltpu.VMEM((2, per, e, t), bf16), pltpu.SemaphoreType.DMA((count, 8)), pltpu.SemaphoreType.DMA((2,))]
    if fold:
        scratch.append(pltpu.VMEM((count * per, 8, t), f32))
    return order.call(
        partial(attend_back_kernel, head_size, fold, first, count, len(earlier)),
        out_shape=out_shape,
        in_specs=[VM] + [HBM] * (5 + len(earlier)),
        out_specs=[HBM] * len(out_shape),
        input_output_aliases={6 + i: i for i in range(len(earlier))},
        scratch_shapes=scratch,
        vmem=32,
        name="attend_back",
    )(inverse, probs, grad_mixed, queries, keys, values, *earlier)


def terms_kernel(count, place, *refs):
    lefts, rights, out = refs[:count], refs[count : 2 * count], refs[2 * count]
    v_lefts, v_rights, sent, sems = refs[2 * count + 1 : 3 * count + 1], refs[3 * count + 1 : 4 * count + 1], refs[-2], refs[-1]
    rows = out.shape[2]
    moves = Moves(sems)
    lanes = half_lanes(1 - place[0], 2 * rows)
    got = [(moves.load(lefts[u], v_lefts[u]), moves.load(rights[u].at[:, lanes], v_rights[u])) for u in range(count)]
    for u in range(count):
        here = pl.ds(u * rows, rows)
        for copy in got[u]:
            copy.wait()
        for b in range(2):
            sent[b, here, :] = dot(v_lefts[u][:, b * rows : (b + 1) * rows], v_rights[u][...], TN)
            moves.store(sent.at[b, here], out.at[b, here])
    moves.finish()


def terms(order, place, lefts, rights):
    count = len(lefts)
    d = lefts[0].shape[1]
    out = (2, count * (d // 2), d // 2)
    return order.call(
        partial(terms_kernel, count),
        out_shape=shaped(out, f32),
        in_specs=[SM] + [HBM] * (2 * count),
        out_specs=HBM,
        scratch_shapes=[pltpu.VMEM(x.shape, bf16) for x in lefts]
        + [pltpu.VMEM((x.shape[0], d // 2), bf16) for x in rights]
        + [pltpu.VMEM(out, f32), pltpu.SemaphoreType.DMA((4 * count,))],
        vmem=24,
        name="terms",
    )(place, *lefts, *rights)


def terms_kept_kernel(count, axes, place, *refs):
    lefts, rights = refs[:count], refs[count : 2 * count]
    sent, o_send, o_keep = refs[2 * count : 2 * count + 3]
    v_lefts, v_rights = refs[2 * count + 3 : 3 * count + 3], refs[3 * count + 3 : 4 * count + 3]
    v_sent, full, sems = refs[4 * count + 3 :]
    rows = sent.shape[2]
    moves = Moves(sems)
    lanes = half_lanes(place[0], 2 * rows)
    got = []
    for u in range(count):
        here = pl.ds(u * rows, rows)
        got.append(
            (
                moves.load(lefts[u], v_lefts[u]),
                moves.load(rights[u].at[:, lanes], v_rights[u]),
                moves.load(sent.at[:, here], v_sent.at[:, here]),
            )
        )
    for u in range(count):
        here = slice(u * rows, (u + 1) * rows)
        for copy in got[u]:
            copy.wait()
        for b in range(2):
            full[b, here, :] = v_sent[b, here, :] + dot(v_lefts[u][:, b * rows : (b + 1) * rows], v_rights[u][...], TN)
    cut_first(axes, place, full, o_send, o_keep)


def terms_kept(order, axes, place, lefts, rights, sent):
    count = len(lefts)
    d = lefts[0].shape[1]
    return order.call(
        partial(terms_kept_kernel, count, axes),
        out_shape=[shaped(sent.shape[1:], f32)] * 2,
        in_specs=[SM] + [HBM] * (2 * count) + [ANY],
        out_specs=[VM] * 2,
        scratch_shapes=[pltpu.VMEM(x.shape, bf16) for x in lefts]
        + [pltpu.VMEM((x.shape[0], d // 2), bf16) for x in rights]
        + [pltpu.VMEM(sent.shape, f32), pltpu.VMEM(sent.shape, f32), pltpu.SemaphoreType.DMA((3 * count,))],
        vmem=30,
        name="terms_kept",
    )(place, *lefts, *rights, sent)


def cross_close_kernel(
    rows, grad_two, stream1, dq, cq, wo, o_grad, o_low, o_mixed, o_gain,
    v_two, v_stream, v_dq, v_cq, v_wo, grad, low, mixed, sems,
):
    moves = Moves(sems)
    sources = (dq, cq, stream1, grad_two, wo)
    got = [moves.load(s, t) for s, t in zip(sources, (v_dq, v_cq, v_stream, v_two, v_wo))]
    for copy in got[:2]:
        copy.wait()
    back = dot(v_dq[...], v_cq[...], NT)
    for copy in got[2:4]:
        copy.wait()
    pulled, gain_grad = norm_pull(back, v_stream[...], rows[1:2, :])
    o_gain[...] = gain_grad
    grad[...] = v_two[...] + pulled
    moves.store(grad, o_grad)
    low[...] = grad[...].astype(bf16)
    moves.store(low, o_low)
    got[4].wait()
    mixed[...] = dot(low[...], v_wo[...], NT).astype(bf16)
    moves.store(mixed, o_mixed)
    moves.finish()


def cross_close(order, rows, grad_two, stream1, dq, cq, wo):
    t, d = dq.shape
    td, dd = (t, d), (d, d)
    return order.call(
        cross_close_kernel,
        out_shape=[shaped(td, f32), shaped(td, bf16), shaped(td, bf16), shaped((1, d), f32)],
        in_specs=[VM] + [HBM] * 5,
        out_specs=[HBM] * 3 + [VM],
        scratch_shapes=[pltpu.VMEM(td, f32), pltpu.VMEM(td, f32)]
        + [pltpu.VMEM(s, bf16) for s in (td, dd, dd)]
        + [pltpu.VMEM(td, f32), pltpu.VMEM(td, bf16), pltpu.VMEM(td, bf16)]
        + [pltpu.SemaphoreType.DMA((8,))],
        vmem=20,
        name="cross_close",
    )(rows, grad_two, stream1, dq, cq, wo)


def enc_close_kernel(dk, dv, ck, cv, out, v_dk, v_dv, v_ck, v_cv, total, sems):
    moves = Moves(sems)
    got = [moves.load(s, t) for s, t in ((dk, v_dk), (ck, v_ck), (dv, v_dv), (cv, v_cv))]
    for copy in got:
        copy.wait()
    rows = out.shape[0] // 2
    for i in range(2):
        here = pl.ds(i * rows, rows)
        total[here, :] = dot(v_dk[here, :], v_ck[...], NT) + dot(v_dv[here, :], v_cv[...], NT)
        moves.store(total.at[here], out.at[here])
    moves.finish()


def enc_close(order, dk, dv, ck, cv):
    e, d = dk.shape
    return order.call(
        enc_close_kernel,
        out_shape=shaped((e, d), f32),
        in_specs=[HBM] * 4,
        out_specs=HBM,
        scratch_shapes=[pltpu.VMEM((e, d), bf16)] * 2
        + [pltpu.VMEM((d, d), bf16)] * 2
        + [pltpu.VMEM((e, d), f32), pltpu.SemaphoreType.DMA((6,))],
        vmem=20,
        name="enc_close",
    )(dk, dv, ck, cv)


def self_close_kernel(
    table_shape, flag, rows, gain_b, gain_c, grad_one, dec, dq, dk, dv, dist, wq, wk, wv, o_grad, o_small,
    v_one, v_dec, v_dq, v_dk, v_dv, v_dist, v_wq, v_wk, v_wv, grad_zero, sems,
):
    t, d = dq.shape
    heads = dist.shape[0]
    num_buckets = table_shape[0]
    moves = Moves(sems)
    sources = (dq, wq, dk, wk, dv, wv, dec, grad_one, dist)
    targets = (v_dq, v_wq, v_dk, v_wk, v_dv, v_wv, v_dec, v_one, v_dist)
    got = [moves.load(s, t_) for s, t_ in zip(sources, targets)]
    dir_row = jnp.where(flag[0] == 0, rows[3:4, :], rows[4:5, :])
    back = None
    for i, (grad, weight) in enumerate(((v_dq, v_wq), (v_dk, v_wk), (v_dv, v_wv))):
        got[2 * i].wait()
        got[2 * i + 1].wait()
        term = dot(grad[...], weight[...], NT)
        back = term if back is None else back + term
    got[6].wait()
    got[7].wait()
    pulled, gain_grad = norm_pull(back, v_dec[...].astype(f32) + dir_row, rows[0:1, :])
    grad_zero[...] = v_one[...] + pulled
    moves.store(grad_zero, o_grad)
    row_sum = jnp.sum(grad_zero[...], axis=0, keepdims=True)
    picked = (flag[0] == 0).astype(f32)
    o_small[...] = jnp.zeros(o_small.shape, f32)
    o_small[0:1, :] = gain_grad
    o_small[1:2, :] = gain_b[...]
    o_small[2:3, :] = gain_c[...]
    o_small[3:4, :] = row_sum * picked
    o_small[4:5, :] = row_sum * (1.0 - picked)
    pick = lax.broadcasted_iota(jnp.int32, (num_buckets, t), 0).astype(f32) == rows[5:6, :t]
    got[8].wait()
    per_head = [jnp.sum(v_dist[h], axis=0, keepdims=True) for h in range(heads)]
    per_head += [jnp.zeros((1, t), f32)] * (-heads % 8)
    table = lax.dot_general(
        jnp.where(pick, 1.0, 0.0).astype(f32),
        jnp.concatenate(per_head, axis=0),
        NT,
        precision=lax.Precision.HIGHEST,
        preferred_element_type=f32,
    )
    o_small[8:, 0 : table.shape[1]] = table
    moves.finish()


def self_close(order, table_shape, flag, rows, gain_b, gain_c, grad_one, dec, dq, dk, dv, dist, wq, wk, wv):
    t, d = dq.shape
    td, dd = (t, d), (d, d)
    return order.call(
        partial(self_close_kernel, table_shape),
        out_shape=[shaped(td, f32), shaped((8 + table_shape[0], d), f32)],
        in_specs=[SM, VM, VM, VM] + [HBM] * 9,
        out_specs=[HBM, VM],
        scratch_shapes=[pltpu.VMEM(td, f32)]
        + [pltpu.VMEM(td, bf16)] * 4
        + [pltpu.VMEM(dist.shape, f32)]
        + [pltpu.VMEM(dd, bf16)] * 3
        + [pltpu.VMEM(td, f32), pltpu.SemaphoreType.DMA((10,))],
        vmem=24,
        name="self_close",
    )(flag, rows, gain_b, gain_c, grad_one, dec, dq, dk, dv, dist, wq, wk, wv)


class Links:
    def __init__(self, dp, rep):
        self.dp, self.rep = dp, rep
        self.lines = dp // 4

    def send(self, value, target):
        pairs = []
        for i in range(self.dp):
            for r in range(self.rep):
                line, side, core, to_rep = target(i // 4, i // 2 % 2, i % 2, r)
                pairs.append((i * self.rep + r, ((line * 2 + side) * 2 + core) * self.rep + to_rep))
        return lax.ppermute(value, ("dp", "rep"), pairs)

    def core(self, value):
        return self.send(value, lambda line, side, core, r: (line, side, core ^ 1, r))

    def line(self, value, flip):
        return self.send(value, lambda line, side, core, r: (line ^ flip, side, core, r))

    def swap(self, value, axes):
        def target(line, side, core, r):
            axis = axes[core]
            return line ^ (axis == "z"), side ^ (axis == "x"), core, r ^ (axis == "y")

        return self.send(value, target)

    def line_flips(self, first):
        flips = []
        while first < self.lines:
            flips.append(first)
            first *= 2
        return flips


def mebibytes(*arrays):
    return 2 + sum(-(-math.prod(a.shape) * 4 // 2**20) for a in arrays)


def add(order, a, b):
    def kernel(left, right, out):
        out[...] = left[...] + right[...]

    return order.call(
        kernel,
        in_specs=[VM, VM],
        out_specs=VM,
        out_shape=shaped(a.shape, f32),
        vmem=mebibytes(a, b, a),
        name="add",
    )(a, b)


def split_add(order, axes, place, keep, got):
    keep, got = (x.reshape((2, -1, x.shape[-1])) for x in (keep, got))

    def kernel(at, left, right, o_send, o_mine):
        mine = bit_of(at, axes)
        o_send[...] = left[1 - mine] + right[1 - mine]
        o_mine[...] = left[mine] + right[mine]

    return order.call(
        kernel,
        in_specs=[SM, VM, VM],
        out_specs=[VM, VM],
        out_shape=[shaped(keep.shape[1:], f32)] * 2,
        vmem=mebibytes(keep, got, keep),
        name="split_add",
    )(place, keep, got)


def join(order, axes, place, mine, far):
    def kernel(at, left, right, out):
        bit = bit_of(at, axes)
        out[bit] = left[...]
        out[1 - bit] = right[...]

    out = order.call(
        kernel,
        in_specs=[SM, VM, VM],
        out_specs=VM,
        out_shape=shaped((2,) + mine.shape, f32),
        vmem=mebibytes(mine, far, mine, far),
        name="join",
    )(place, mine, far)
    return out.reshape((-1, mine.shape[-1]))


def sum_bundle(order, links, place, ways, send, keep):
    steps = list(zip(*ways))
    back = list(zip(*([axis for axis in reversed(way) if axis != "y"] for way in ways)))
    got = links.swap(send, steps[0])
    yield
    for axes in steps[1:]:
        send, keep = split_add(order, axes, place, keep, got)
        got = links.swap(send, axes)
        yield
    mine = add(order, keep, got)
    for flip in links.line_flips(2):
        got = links.line(mine, flip)
        yield
        mine = add(order, mine, got)
    for axes in back:
        got = links.swap(mine, axes)
        yield
        mine = join(order, axes, place, mine, got)
    got = links.core(mine)
    yield
    return mine, got


def place_kernel(segments, aliased, place, mine, other, *refs):
    outs, sems = refs[aliased:-1], refs[-1]
    copies = []
    for i, (piece, core) in enumerate(((mine, place[0]), (other, 1 - place[0]))):
        for j, (first, count, out, row, base, step) in enumerate(segments):
            lanes = pl.ds(pl.multiple_of(base + core * step, LANES), piece.shape[1])
            copies.append(
                pltpu.make_async_copy(piece.at[pl.ds(first, count)], outs[out].at[pl.ds(row, count), lanes], sems.at[i, j])
            )
    for copy in copies:
        copy.start()
    for copy in copies:
        copy.wait()


def place_pieces(order, place, pieces, segments, out_shapes, aliased=()):
    return order.call(
        partial(place_kernel, segments, len(aliased)),
        in_specs=[SM, VM, VM] + [HBM] * len(aliased),
        out_specs=[HBM] * len(out_shapes),
        out_shape=out_shapes,
        input_output_aliases={3 + i: i for i in range(len(aliased))},
        scratch_shapes=[pltpu.SemaphoreType.DMA((2, len(segments)))],
        vmem=mebibytes(*pieces[:2]),
        name="place",
    )(place, *pieces, *aliased)


def sum_small(order, links, small):
    for axes in ("yy", "xx", "zz"):
        got = links.swap(small, axes)
        yield
        small = add(order, small, got)
    for flip in links.line_flips(2):
        got = links.line(small, flip)
        yield
        small = add(order, small, got)
    got = links.core(small)
    yield
    return add(order, small, got)


class Live:
    def __init__(self, steps):
        self.steps, self.result = steps, None
        self.step()

    def step(self):
        if self.result is None:
            try:
                next(self.steps)
            except StopIteration as end:
                self.result = end.value

    def finish(self):
        while self.result is None:
            self.step()
        return self.result


PLAN = (
    "fwd", "feed0", "feed1", "kept0", "result", "kept1", "close", "attb0", "F0", "attb1", "cterm0", "F1", "enc", "F0",
    "ckept0", "cclose", "F1", "F0", "atta0", "oterm0", "C0", "F1", "oterm1", "okept0", "F0", "okept1", "C0", "O0",
    "F0", "F1", "C0", "O1", "F1", "O0", "F0", "C0", "F0p", "O0", "O1", "sclose", "C0", "S", "O0", "F1", "O1", "O0",
    "F1p", "O1", "C0", "S", "O1", "S", "C0p", "S", "O0", "S", "O0p", "O1", "O1p",
)
FEED_CUTS = (2, 2)
FEED_WAYS = (("yxz", "xyz"), ("yxz", "xyz"))
CROSS_WAYS = (("yxz", "xyz"),)
OWN_WAYS = (("yxz", "xyz"), ("yxz", "yxz"))
ATTEND = (2, 1)


def local(
    dp, rep,
    dec_input, enc_states, out_cotangent, dec_lengths, group_ids, direction_flags, rel_buckets, step_index,
    self_gain, self_query, self_key, self_value, self_output, bucket_bias_table,
    cross_gain, cross_query, cross_key, cross_value, cross_output, feed_gain, feed_inner, feed_outer, dir_table,
):
    dec, enc, cot = dec_input[0], enc_states[0], out_cotangent[0]
    num_buckets, num_heads = bucket_bias_table.shape
    d = dec.shape[1]
    half = d // 2
    head_size = d // num_heads
    pairs = d // LANES
    links = Links(dp, rep)
    dp_index, rep_index = lax.axis_index("dp"), lax.axis_index("rep")
    place = jnp.stack([dp_index % 2, rep_index, (dp_index // 4) % 2, (dp_index // 2) % 2]).astype(jnp.int32)
    phase = full_turn * step_index.astype(f32) / PERIOD
    weight = 1.0 + 0.5 * jnp.cos(phase + full_turn * group_ids.astype(f32) / 3.0)
    length, flag = dec_lengths, direction_flags
    order = Order()
    env = {}
    live = {}
    block = feed_inner.shape[1] // 2
    starts = [sum(FEED_CUTS[:i]) for i in range(len(FEED_CUTS))]
    cuts = tuple((a * half, n * half) for a, n in zip(starts, FEED_CUTS))
    actives, pulls, sents = {}, {}, {}
    outer_shape = shaped((feed_outer.shape[0] // rep, d), f32)
    inner_shape = shaped((d // rep, feed_inner.shape[1]), f32)
    feed_grads = []
    done = {}

    def run_forward():
        names = (
            "input_a", "q", "k", "v", "mixed_a", "stream1", "input_b", "xq", "ek", "ev", "mixed_b", "stream2", "input_c",
            "probs_a", "probs_b", "rows", "inv_a", "inv_b",
        )
        smalls = (self_gain, cross_gain, feed_gain, dir_table, rel_buckets, bucket_bias_table.T)
        weights = (self_query, self_key, self_value, self_output, cross_query, cross_key, cross_value, cross_output)
        env.update(zip(names, forward(order, head_size, num_buckets, flag, smalls, dec, enc, weights)))

    def run_feed(p):
        actives[p], pulls[p], sent = feed(order, *cuts[p], place, weight, length, cot, env["input_c"], feed_inner, feed_outer)
        sents[p] = links.core(sent)

    def run_kept(p):
        first = [way[0] for way in FEED_WAYS[p]]
        send, keep = feed_kept(order, first, place, weight, length, cot, env["input_c"], actives[p], pulls[p], sents[p])
        live[f"F{p}"] = Live(sum_bundle(order, links, place, FEED_WAYS[p], send, keep))

    def run_close():
        pulled = [pulls[i] for i in range(len(cuts))]
        outs = close(order, cuts, weight, length, env["rows"], cot, env["stream2"], pulled, feed_inner, cross_output)
        env.update(zip(("grad_two", "low_two", "grad_mixed_b", "gain_c_grad"), outs))

    def run_result():
        active = [actives[i] for i in range(len(cuts))]
        env["block_output"] = block_result(order, cuts, length, env["stream2"], active, feed_outer)

    def run_attend(i, groups, fold, name, *args):
        count = pairs // groups
        env[name] = attend_back(order, head_size, fold, i * count, count, *(env[a] for a in args), earlier=env.get(name, ()))

    def run_cross_close():
        outs = cross_close(
            order, env["rows"], env["grad_two"], env["stream1"], env["back_b"][0], cross_query, self_output
        )
        env.update(zip(("grad_one", "low_one", "grad_mixed_a", "gain_b_grad"), outs))

    def run_enc_close():
        env["enc_grad"] = enc_close(order, *env["back_b"][1:], cross_key, cross_value)

    def run_self_close():
        outs = self_close(
            order, bucket_bias_table.shape, flag, env["rows"], env["gain_b_grad"], env["gain_c_grad"], env["grad_one"], dec,
            *env["back_a"], self_query, self_key, self_value,
        )
        env["input_grad"], small = outs
        live["S"] = Live(sum_small(order, links, small))

    def operands(own):
        if own:
            dq, dk, dv, _ = env["back_a"]
            return (env["mixed_a"], env["input_a"], env["input_a"], env["input_a"]), (env["low_one"], dq, dk, dv)
        dq, dk, dv = env["back_b"]
        return (env["mixed_b"], env["input_b"], enc, enc), (env["low_two"], dq, dk, dv)

    def piece(own, i):
        count = 4 // len(OWN_WAYS if own else CROSS_WAYS)
        return [x[i * count : (i + 1) * count] for x in operands(own)]

    def run_terms(own, i):
        sents[own, i] = links.core(terms(order, place, *piece(own, i)))

    def run_terms_kept(own, i):
        ways = (OWN_WAYS if own else CROSS_WAYS)[i]
        send, keep = terms_kept(order, [way[0] for way in ways], place, *piece(own, i), sents[own, i])
        live[f"{'O' if own else 'C'}{i}"] = Live(sum_bundle(order, links, place, ways, send, keep))

    def run_place(name):
        pieces = live[name].finish()
        if name[0] == "F":
            offset, split = cuts[int(name[1:])]
            segments = [(0, split, 0, offset, 0, half)]
            segments += [(split + i * half, half, 1, 0, offset + i * half, block) for i in range(split // half)]
            feed_grads[:] = place_pieces(order, place, pieces, segments, [outer_shape, inner_shape], feed_grads)
        else:
            count = 4 // len(OWN_WAYS if name[0] == "O" else CROSS_WAYS)
            segments = [(j * half, half, j, 0, 0, half) for j in range(count)]
            done[name] = place_pieces(order, place, pieces, segments, [shaped((half, d), f32)] * count)

    for name in PLAN:
        head = name.rstrip("0123456789p")
        index = int(name[len(head)]) if name[-1].isdigit() else None
        if name == "fwd":
            run_forward()
        elif head == "feed":
            run_feed(index)
        elif head == "kept":
            run_kept(index)
        elif name == "close":
            run_close()
        elif name == "result":
            run_result()
        elif name == "enc":
            run_enc_close()
        elif head == "attb":
            run_attend(index, ATTEND[0], False, "back_b", "inv_b", "probs_b", "grad_mixed_b", "xq", "ek", "ev")
        elif head == "atta":
            run_attend(index, ATTEND[1], True, "back_a", "inv_a", "probs_a", "grad_mixed_a", "q", "k", "v")
        elif name == "cclose":
            run_cross_close()
        elif name == "sclose":
            run_self_close()
        elif head in ("oterm", "cterm"):
            run_terms(head == "oterm", index)
        elif head in ("okept", "ckept"):
            run_terms_kept(head == "okept", index)
        elif name.endswith("p"):
            run_place(name[:-1])
        else:
            live[name].step()

    outer, inner = feed_grads
    small = live["S"].finish()
    cross = [x for i in range(len(CROSS_WAYS)) for x in done[f"C{i}"]]
    own = [x for i in range(len(OWN_WAYS)) for x in done[f"O{i}"]]
    small_rows = lambda i: lax.dynamic_slice_in_dim(small[i], rep_index * half, half)
    table_rows = num_buckets // rep
    table = lax.dynamic_slice(small, (8 + rep_index * table_rows, 0), (table_rows, num_heads))
    dir_grad = lax.dynamic_slice_in_dim(small, 3 + rep_index, 1)
    return (
        env["block_output"][None],
        env["input_grad"][None],
        env["enc_grad"][None],
        small_rows(0),
        own[1],
        own[2],
        own[3],
        own[0],
        table,
        small_rows(1),
        cross[1],
        cross[2],
        cross[3],
        cross[0],
        small_rows(2),
        inner,
        outer,
        dir_grad,
    )


def solution(mesh):
    pair = P(("dp", "rep"), None, None)
    each = P(("dp", "rep"))
    rows = P("rep", None)
    vector = P("rep")
    return jax.shard_map(
        partial(local, mesh.shape["dp"], mesh.shape["rep"]),
        mesh=mesh,
        in_specs=(pair, pair, pair, each, each, each) + (P(),) * 17,
        out_specs=(
            pair, pair, pair, vector, rows, rows, rows, rows, rows, vector, rows, rows, rows, rows, vector, rows, rows, rows,
        ),
        check_vma=False,
    )
```

```python
from functools import partial
import math

import jax
import jax.numpy as jnp
from jax import lax
from jax.experimental import pallas as pl
from jax.experimental.pallas import tpu as pltpu
from jax.sharding import PartitionSpec as P

PERIOD = 1000
full_turn = 2.0 * math.pi
norm_eps = 1e-06
masked_score = -1e30
LANES = 128
FLOPS = 2 * 10**10
BYTES = 10**7
f32 = jnp.float32
bf16 = jnp.bfloat16

NN = (((1,), (0,)), ((), ()))
NT = (((1,), (1,)), ((), ()))
TN = (((0,), (0,)), ((), ()))


def dot(left, right, form):
    return lax.dot_general(left, right, form, preferred_element_type=f32)


def shaped(shape, dtype):
    return jax.ShapeDtypeStruct(shape, dtype)


class Order:
    def __init__(self):
        self.last, self.held = None, False

    def call(self, kernel, *, in_specs, out_shape, out_specs, vmem, **more):
        count = len(in_specs)
        held = lambda shape, spec: pltpu.HBM(shape.shape, shape.dtype) if spec is HBM else shape
        if isinstance(out_specs, list):
            out_shape = [held(a, b) for a, b in zip(out_shape, out_specs)]
        else:
            out_shape = held(out_shape, out_specs)

        def apply(*args):
            after = [] if self.last is None or any(self.last is a for a in args) else [self.last]
            if self.held:
                after = [pltpu.with_memory_space_constraint(a, pltpu.HBM) for a in after]

            def ordered(*refs):
                return kernel(*refs[:count], *refs[count + len(after) :])

            args = [
                pltpu.with_memory_space_constraint(a, pltpu.HBM) if s is HBM or s is FROM_HBM else a
                for a, s in zip(args, in_specs)
            ]
            outs = pl.pallas_call(
                ordered,
                in_specs=list(in_specs) + [ANY] * len(after),
                out_shape=out_shape,
                out_specs=out_specs,
                compiler_params=pltpu.CompilerParams(vmem_limit_bytes=vmem * 2**20),
                cost_estimate=pl.CostEstimate(flops=FLOPS, bytes_accessed=BYTES, transcendentals=0),
                **more,
            )(*args, *after)
            self.last, self.held = jax.tree.leaves(outs)[0], jax.tree.leaves(out_specs)[0] is HBM
            return outs

        return apply


HBM = pl.BlockSpec(memory_space=pltpu.HBM)
ANY = pl.BlockSpec(memory_space=pl.ANY)
VM = pl.BlockSpec(memory_space=pltpu.VMEM)
FROM_HBM = pl.BlockSpec(memory_space=pltpu.VMEM)
SM = pl.BlockSpec(memory_space=pltpu.SMEM)
AXES = {"y": 1, "z": 2, "x": 3}


class Moves:
    def __init__(self, sems):
        self.sems, self.count, self.stores = sems, 0, []

    def load(self, source, target):
        copy = pltpu.make_async_copy(source, target, self.sems.at[self.count])
        self.count += 1
        copy.start()
        return copy

    def store(self, source, target):
        self.stores.append(self.load(source, target))

    def finish(self):
        for copy in self.stores:
            copy.wait()


def norm_rows(stream, gain):
    scale = lax.rsqrt(jnp.mean(stream * stream, axis=-1, keepdims=True) + norm_eps)
    return stream * scale * gain


def norm_pull(grad_out, stream, gain):
    scale = lax.rsqrt(jnp.mean(stream * stream, axis=-1, keepdims=True) + norm_eps)
    normed = stream * scale
    gain_grad = jnp.sum(grad_out * normed, axis=0, keepdims=True)
    grad_normed = grad_out * gain
    inner_mean = jnp.mean(grad_normed * normed, axis=-1, keepdims=True)
    return scale * (grad_normed - normed * inner_mean), gain_grad


def weighted(cot, length, weight):
    valid = (lax.broadcasted_iota(jnp.int32, (cot.shape[0], 1), 0) < length[0]).astype(f32)
    return valid, valid * (cot[...].astype(f32) * weight[0])


def head_masks(width, head_size):
    lane = lax.broadcasted_iota(jnp.int32, (1, width), 1)
    return [jnp.where(lane // head_size == i, 1.0, 0.0).astype(f32) for i in range(width // head_size)]


def pair_lanes(index):
    return pl.ds(pl.multiple_of(index * LANES, LANES), LANES)


def half_lanes(half, width):
    return pl.ds(pl.multiple_of(half * (width // 2), LANES), width // 2)


def forward_kernel(
    head_size, num_buckets,
    flag, self_gain, cross_gain, feed_gain, dirs, buckets, table, dec, enc, wq, wk, wv, wo, cq, ck, cv, co,
    o_input_a, o_q, o_k, o_v, o_mixed_a, o_stream1, o_input_b, o_cq, o_ek, o_ev, o_mixed_b, o_stream2, o_input_c,
    o_pa, o_pb, o_exact_a, o_exact_b, rows, o_inv_a, o_inv_b,
    v_dec, v_enc, v_wq, v_wk, v_wv, v_wo, v_cq, v_ck, v_cv, v_co,
    input_a, q, k, v, mixed_a, stream1, input_b, xq, ek, ev, mixed_b, stream2, input_c,
    exact_a, exact_b, dist, slots_a, slots_b, sems, slot_sems,
):
    dec_len, width = dec.shape
    pairs = width // LANES
    per = LANES // head_size
    moves = Moves(sems)
    names = (v_dec, v_wq, v_wk, v_wv, v_enc, v_ck, v_cv, v_wo, v_cq, v_co)
    loads = [moves.load(s, t) for s, t in zip((dec, wq, wk, wv, enc, ck, cv, wo, cq, co), names)]
    flat = lambda ref: ref[...].astype(f32).reshape(1, ref.shape[0])
    gain_a, gain_b, gain_c = flat(self_gain), flat(cross_gain), flat(feed_gain)
    rows[...] = jnp.zeros(rows.shape, f32)
    for i, row in enumerate((gain_a, gain_b, gain_c)):
        rows[i : i + 1, :] = row
    rows[3:5, :] = dirs[...].astype(f32)
    rows[5:6, 0:dec_len] = flat(buckets)
    pick = lax.broadcasted_iota(jnp.int32, (num_buckets, dec_len), 0).astype(f32) == rows[5:6, :dec_len]
    dist[0 : table.shape[0], :] = dot(table[...], jnp.where(pick, 1.0, 0.0).astype(bf16), NN)
    dir_row = jnp.where(flag[0] == 0, rows[3:4, :], rows[4:5, :])
    loads[0].wait()
    input_a[...] = norm_rows(v_dec[...].astype(f32) + dir_row, gain_a).astype(bf16)
    moves.store(input_a, o_input_a)
    for load, weight, target, out in ((1, v_wq, q, o_q), (2, v_wk, k, o_k), (3, v_wv, v, o_v)):
        loads[load].wait()
        target[...] = dot(input_a[...], weight[...], NN).astype(bf16)
        moves.store(target, out)
    loads[4].wait()
    for load, weight, target, out in ((5, v_ck, ek, o_ek), (6, v_cv, ev, o_ev)):
        loads[load].wait()
        target[...] = dot(v_enc[...], weight[...], NN).astype(bf16)
        moves.store(target, out)
    masks = head_masks(LANES, head_size)
    edge = dec_len // 2
    key_pos = lax.broadcasted_iota(jnp.int32, (edge, edge), 0)
    query_pos = lax.broadcasted_iota(jnp.int32, (edge, edge), 1)

    def attend(queries, keys, values, mixed, exact_mix, slots, out, inverse, head_rows):
        def slot_copy(index, slot):
            return pltpu.make_async_copy(slots.at[slot], out.at[pl.ds(index * per, per)], slot_sems.at[slot])

        def sweep(by_top):
            def body(index, bounds):
                slot = lax.rem(index, 2)

                @pl.when(index >= 2)
                def _():
                    slot_copy(index - 2, slot).wait()

                lanes = pair_lanes(index)
                key_block, value_rows, query_block = keys[:, lanes], values[:, lanes].T, queries[:, lanes]
                ones = jnp.ones((16, value_rows.shape[1]), bf16)
                parts, sums = [], []
                least, most = bounds
                for i in range(per):
                    mix = jnp.concatenate([value_rows[i * head_size : (i + 1) * head_size], ones], axis=0)
                    total = head_rows(by_top, index, i, slot, key_block, query_block * masks[i].astype(bf16), mix)
                    norm = total[head_size : head_size + 1, :]
                    least, most = jnp.minimum(least, norm), jnp.maximum(most, norm)
                    inv = 1.0 / norm
                    parts.append(total[0:head_size, :] * inv)
                    sums.append(inv)
                both = jnp.concatenate(parts, axis=0).T
                exact_mix[:, lanes] = both
                mixed[:, lanes] = both.astype(bf16)
                inverse[pl.ds(index, 1)] = jnp.concatenate(sums, axis=0)[None]
                slot_copy(index, slot).start()
                return least, most

            bounds = lax.fori_loop(0, pairs, body, (jnp.ones((1, dec_len), f32), jnp.ones((1, dec_len), f32)))
            for index in range(max(pairs - 2, 0), pairs):
                slot_copy(index, index % 2).wait()
            return bounds

        least, most = sweep(False)
        safe = jnp.logical_and(jnp.min(least) > 1e-15, jnp.max(most) < 1e15)

        @pl.when(jnp.logical_not(safe))
        def _():
            sweep(True)

    def raised(scores, top):
        return jnp.exp(scores if top is None else scores - top).astype(bf16)

    def top_of(by_top, *blocks):
        if not by_top:
            return None
        tops = [jnp.max(x, axis=0, keepdims=True) for x in blocks]
        return tops[0] if len(tops) == 1 else jnp.maximum(*tops)

    def own_rows(by_top, index, i, slot, key_block, query, mix):
        row = dist[pl.ds(index * per + i, 1), :]
        bias = pltpu.roll(jnp.broadcast_to(row, (edge, dec_len)), 0, 1, stride=1, stride_axis=0)
        seen = key_pos <= query_pos
        low, high = slice(0, edge), slice(edge, dec_len)
        near = jnp.where(seen, dot(key_block[low], query[low], NT) + bias[:, low], masked_score)
        first = raised(near, top_of(by_top, near))
        slots_a[slot, i, low, low] = first
        far = dot(key_block[low], query[high], NT) + bias[:, high]
        near = jnp.where(seen, dot(key_block[high], query[high], NT) + bias[:, low], masked_score)
        top = top_of(by_top, far, near)
        second, third = raised(far, top), raised(near, top)
        slots_a[slot, i, low, high] = second
        slots_a[slot, i, high, high] = third
        right = dot(mix[:, low], second, NN) + dot(mix[:, high], third, NN)
        return jnp.concatenate([dot(mix[:, low], first, NN), right], axis=1)

    def cross_rows(by_top, index, i, slot, key_block, query, mix):
        scores = dot(key_block, query, NT)
        low = raised(scores, top_of(by_top, scores))
        slots_b[slot, i] = low
        return dot(mix, low, NN)

    attend(q, k, v, mixed_a, exact_a, slots_a, o_pa, o_inv_a, own_rows)
    moves.store(mixed_a, o_mixed_a)
    moves.store(exact_a, o_exact_a)
    loads[7].wait()
    stream1[...] = v_dec[...].astype(f32) + dir_row + dot(mixed_a[...], v_wo[...], NN)
    moves.store(stream1, o_stream1)
    input_b[...] = norm_rows(stream1[...], gain_b).astype(bf16)
    moves.store(input_b, o_input_b)
    loads[8].wait()
    xq[...] = dot(input_b[...], v_cq[...], NN).astype(bf16)
    moves.store(xq, o_cq)
    attend(xq, ek, ev, mixed_b, exact_b, slots_b, o_pb, o_inv_b, cross_rows)
    moves.store(mixed_b, o_mixed_b)
    moves.store(exact_b, o_exact_b)
    loads[9].wait()
    stream2[...] = stream1[...] + dot(mixed_b[...], v_co[...], NN)
    moves.store(stream2, o_stream2)
    input_c[...] = norm_rows(stream2[...], gain_c).astype(bf16)
    moves.store(input_c, o_input_c)
    moves.finish()


def forward(order, head_size, num_buckets, flag, smalls, dec, enc, weights):
    t, d = dec.shape
    e = enc.shape[0]
    heads = d // head_size
    per = LANES // head_size
    td, ed = (t, d), (e, d)
    low = [td, td, td, td, td, None, td, td, ed, ed, td, None, td]
    outs = [shaped(s, bf16) if s else shaped(td, f32) for s in low]
    outs += [shaped((heads, t, t), bf16), shaped((heads, e, t), bf16), shaped(td, f32), shaped(td, f32)]
    outs += [shaped((8, d), f32)]
    outs += [shaped((heads // per, per, t), f32)] * 2
    scratch = [pltpu.VMEM(td, bf16), pltpu.VMEM(ed, bf16)] + [pltpu.VMEM((d, d), bf16)] * 8
    scratch += [pltpu.VMEM(s, bf16) if s else pltpu.VMEM(td, f32) for s in low]
    scratch += [
        pltpu.VMEM(td, f32),
        pltpu.VMEM(td, f32),
        pltpu.VMEM((-(-heads // 8) * 8, t), f32),
        pltpu.VMEM((2, per, t, t), bf16),
        pltpu.VMEM((2, per, e, t), bf16),
        pltpu.SemaphoreType.DMA((25,)),
        pltpu.SemaphoreType.DMA((2,)),
    ]
    return order.call(
        partial(forward_kernel, head_size, num_buckets),
        out_shape=outs,
        in_specs=[SM] + [FROM_HBM] * 6 + [HBM] * 10,
        out_specs=[HBM] * (len(outs) - 3) + [VM] * 3,
        scratch_shapes=scratch,
        vmem=52,
        name="forward",
    )(flag, *smalls, dec, enc, *weights)


def feed_kernel(
    offset, place, weight, length, cot, input_c, w1, w2, o_active, o_pull, o_sent,
    v_cot, v_input, v_w1, v_w2, grad_low, active, pull, sent, sems,
):
    d = cot.shape[1]
    split = v_w1.shape[2]
    block = w1.shape[1] // 2
    rows = d // 2
    moves = Moves(sems)
    columns = [pl.ds(b * block + offset, split) for b in range(2)]
    got_input = moves.load(input_c, v_input)
    got = [[moves.load(w1.at[:, columns[0]], v_w1.at[0])], []]
    got_cot = moves.load(cot, v_cot)
    got[0].append(moves.load(w2.at[columns[0], :], v_w2.at[0]))
    got[1] += [moves.load(w1.at[:, columns[1]], v_w1.at[1]), moves.load(w2.at[columns[1], :], v_w2.at[1])]
    other = 1 - place[0]
    lanes = half_lanes(other, d)
    got_input.wait()
    for b in range(2):
        got[b][0].wait()
        inner = dot(v_input[...], v_w1[b], NN)
        if b == 0:
            got_cot.wait()
            grad_low[...] = weighted(v_cot, length, weight)[1].astype(bf16)
        got[b][1].wait()
        back = dot(grad_low[...], v_w2[b], NT)
        root = math.sqrt(2.0 / math.pi)
        square = inner * inner
        bent = jnp.tanh(root * (inner + 0.044715 * (square * inner)))
        half_up = 0.5 * (1.0 + bent)
        slope = half_up + (0.5 * inner) * (1.0 - bent * bent) * (root * (1.0 + 3.0 * 0.044715 * square))
        active[b] = (inner * half_up).astype(bf16)
        moves.store(active.at[b], o_active.at[b])
        pull[b] = (back * slope).astype(bf16)
        moves.store(pull.at[b], o_pull.at[b])
    for b in range(2):
        sent[b, 0:split, :] = dot(active[b], grad_low[:, lanes], TN)
        for i in range(split // rows):
            sent[b, split + i * rows : split + (i + 1) * rows, :] = dot(
                v_input[:, b * rows : (b + 1) * rows], pull[other, :, i * rows : (i + 1) * rows], TN
            )
        moves.store(sent.at[b], o_sent.at[b])
    moves.finish()


def feed(order, offset, split, place, weight, length, cot, input_c, w1, w2):
    t, d = cot.shape
    wide = (2, t, split)
    out = (2, 2 * split, d // 2)
    return order.call(
        partial(feed_kernel, offset),
        out_shape=[shaped(wide, bf16), shaped(wide, bf16), shaped(out, f32)],
        in_specs=[SM, SM, SM, HBM, HBM, HBM, HBM],
        out_specs=[HBM] * 3,
        scratch_shapes=[
            pltpu.VMEM((t, d), bf16),
            pltpu.VMEM((t, d), bf16),
            pltpu.VMEM((2, d, split), bf16),
            pltpu.VMEM((2, split, d), bf16),
            pltpu.VMEM((t, d), bf16),
            pltpu.VMEM(wide, bf16),
            pltpu.VMEM(wide, bf16),
            pltpu.VMEM(out, f32),
            pltpu.SemaphoreType.DMA((12,)),
        ],
        vmem=32,
        name="feed",
    )(place, weight, length, cot, input_c, w1, w2)


def bit_of(place, axes):
    return jnp.where(place[0] == 0, place[AXES[axes[0]]], place[AXES[axes[1]]])


def cut_first(axes, place, full, out_send, out_keep):
    count = full.shape[1] // 2
    for core in range(2):

        @pl.when(place[0] == core)
        def _(core=core):
            bit = place[AXES[axes[core]]]
            for out, at in ((out_send, 1 - bit), (out_keep, bit)):
                if axes[core] == "y":
                    out[...] = full[at]
                else:
                    for b in range(2):
                        out[b * count : (b + 1) * count, :] = full[b, pl.ds(pl.multiple_of(at * count, 8), count), :]


def feed_kept_kernel(
    axes, place, weight, length, cot, input_c, active, pull, sent, o_send, o_keep,
    v_cot, v_input, v_active, v_pull, v_sent, grad_low, full, sems,
):
    d = cot.shape[1]
    split = active.shape[2]
    rows = d // 2
    half = place[0]
    moves = Moves(sems)
    lanes = half_lanes(half, d)
    got = [moves.load(cot.at[:, lanes], v_cot), moves.load(active, v_active), moves.load(sent, v_sent)]
    got += [moves.load(input_c, v_input), moves.load(pull.at[half], v_pull)]
    got[0].wait()
    grad_low[...] = weighted(v_cot, length, weight)[1].astype(bf16)
    got[1].wait()
    got[2].wait()
    for b in range(2):
        full[b, 0:split, :] = v_sent[b, 0:split, :] + dot(v_active[b], grad_low[...], TN)
    got[3].wait()
    got[4].wait()
    for b in range(2):
        for i in range(split // rows):
            here = slice(split + i * rows, split + (i + 1) * rows)
            full[b, here, :] = v_sent[b, here, :] + dot(
                v_input[:, b * rows : (b + 1) * rows], v_pull[:, i * rows : (i + 1) * rows], TN
            )
    cut_first(axes, place, full, o_send, o_keep)


def feed_kept(order, axes, place, weight, length, cot, input_c, active, pull, sent):
    t, d = cot.shape
    split = active.shape[2]
    return order.call(
        partial(feed_kept_kernel, axes),
        out_shape=[shaped(sent.shape[1:], f32)] * 2,
        in_specs=[SM, SM, SM] + [HBM] * 4 + [ANY],
        out_specs=[VM] * 2,
        scratch_shapes=[
            pltpu.VMEM((t, d // 2), bf16),
            pltpu.VMEM((t, d), bf16),
            pltpu.VMEM((2, t, split), bf16),
            pltpu.VMEM((t, split), bf16),
            pltpu.VMEM(sent.shape, f32),
            pltpu.VMEM((t, d // 2), bf16),
            pltpu.VMEM(sent.shape, f32),
            pltpu.SemaphoreType.DMA((5,)),
        ],
        vmem=30,
        name="feed_kept",
    )(place, weight, length, cot, input_c, active, pull, sent)


def close_kernel(cuts, *refs):
    parts = len(cuts)
    weight, length, rows, cot, stream2 = refs[:5]
    pulls = refs[5 : 5 + parts]
    w1, wo, o_grad, o_low, o_mixed, o_gain, v_cot, v_stream, v_pull, v_w1, v_wo, grad, low, mixed, sems = refs[5 + parts :]
    block = w1.shape[1] // 2
    moves = Moves(sems)
    got = []
    for b in range(2):
        for p, (offset, split) in enumerate(cuts):
            here = pl.ds(b * block + offset, split)
            got.append(moves.load(pulls[p].at[b], v_pull.at[:, here]))
            got.append(moves.load(w1.at[:, here], v_w1.at[:, here]))
    got_stream, got_cot = moves.load(stream2, v_stream), moves.load(cot, v_cot)
    got_wo = moves.load(wo, v_wo)
    back = None
    for b in range(2):
        here = slice(b * block, (b + 1) * block)
        for copy in got[b * 2 * parts : (b + 1) * 2 * parts]:
            copy.wait()
        term = dot(v_pull[:, here], v_w1[:, here], NT)
        back = term if back is None else back + term
    got_stream.wait()
    pulled, gain_grad = norm_pull(back, v_stream[...], rows[2:3, :])
    o_gain[...] = gain_grad
    got_cot.wait()
    grad[...] = pulled + weighted(v_cot, length, weight)[1]
    moves.store(grad, o_grad)
    low[...] = grad[...].astype(bf16)
    moves.store(low, o_low)
    got_wo.wait()
    mixed[...] = dot(low[...], v_wo[...], NT).astype(bf16)
    moves.store(mixed, o_mixed)
    moves.finish()


def close(order, cuts, weight, length, rows, cot, stream2, pulls, w1, wo):
    t, d = cot.shape
    parts = len(cuts)
    td = (t, d)
    return order.call(
        partial(close_kernel, cuts),
        out_shape=[shaped(td, f32), shaped(td, bf16), shaped(td, bf16), shaped((1, d), f32)],
        in_specs=[SM, SM, VM] + [HBM] * (4 + parts),
        out_specs=[HBM] * 3 + [VM],
        scratch_shapes=[
            pltpu.VMEM(td, bf16),
            pltpu.VMEM(td, f32),
            pltpu.VMEM((t, w1.shape[1]), bf16),
            pltpu.VMEM(w1.shape, bf16),
            pltpu.VMEM((d, d), bf16),
            pltpu.VMEM(td, f32),
            pltpu.VMEM(td, bf16),
            pltpu.VMEM(td, bf16),
            pltpu.SemaphoreType.DMA((4 * parts + 6,)),
        ],
        vmem=30,
        name="close",
    )(weight, length, rows, cot, stream2, *pulls, w1, wo)


def result_kernel(cuts, *refs):
    parts = len(cuts)
    length, stream2 = refs[:2]
    actives = refs[2 : 2 + parts]
    w2, out, v_stream, v_active, v_w2, sems = refs[2 + parts :]
    block = w2.shape[0] // 2
    moves = Moves(sems)
    got = []
    for b in range(2):
        for p, (offset, split) in enumerate(cuts):
            here = pl.ds(b * block + offset, split)
            got.append(moves.load(actives[p].at[b], v_active.at[:, here]))
            got.append(moves.load(w2.at[here, :], v_w2.at[here, :]))
    got.append(moves.load(stream2, v_stream))
    for copy in got:
        copy.wait()
    valid = (lax.broadcasted_iota(jnp.int32, (out.shape[0], 1), 0) < length[0]).astype(f32)
    out[...] = (valid * (v_stream[...] + dot(v_active[...], v_w2[...], NN))).astype(bf16)


def block_result(order, cuts, length, stream2, actives, w2):
    t, d = stream2.shape
    parts = len(cuts)
    return order.call(
        partial(result_kernel, cuts),
        out_shape=shaped((t, d), bf16),
        in_specs=[SM] + [HBM] * (2 + parts),
        out_specs=VM,
        scratch_shapes=[
            pltpu.VMEM((t, d), f32),
            pltpu.VMEM((t, w2.shape[0]), bf16),
            pltpu.VMEM(w2.shape, bf16),
            pltpu.SemaphoreType.DMA((4 * parts + 1,)),
        ],
        vmem=24,
        name="result",
    )(length, stream2, *actives, w2)


def fold_diagonals(tiles):
    count, length = tiles.shape
    steps = LANES // 8
    total = None
    for u in range(steps):
        acc = None
        for k in range(count // LANES):
            t = k * steps + u
            tile = tiles[8 * t : 8 * t + 8, :]
            if k:
                tile = jnp.concatenate([tile[:, LANES * k :], tile[:, : LANES * k]], axis=1)
            acc = tile if acc is None else acc + tile
        if u:
            acc = pltpu.roll(acc, length - 8 * u, 1)
        total = acc if total is None else total + acc
    rows = lax.broadcasted_iota(jnp.int32, (8, length), 0)
    for b in (1, 2, 4):
        total = jnp.where((rows & b) != 0, pltpu.roll(total, length - b, 1), total)
    return total


def attend_back_kernel(
    head_size, fold, first, count, earlier, inverse, probs, exact_mix, grad_mixed, queries, keys, values, *refs
):
    refs = refs[earlier:]
    o_q, o_k, o_v = refs[:3]
    o_dist = refs[3] if fold else None
    v_mix, v_grad, v_q, v_k, v_v, v_dq, v_dk, v_dv, slots, sems, slot_sems = refs[3 + fold : 14 + fold]
    v_dist = refs[14 + fold] if fold else None
    per = LANES // head_size
    masks = head_masks(LANES, head_size)

    def there(index):
        return pl.ds(pl.multiple_of((first + index) * LANES, LANES), LANES)

    def pair_loads(index):
        both = zip((values, grad_mixed, exact_mix, keys, queries), (v_v, v_grad, v_mix, v_k, v_q))
        return [
            pltpu.make_async_copy(s.at[:, there(index)], t.at[:, pair_lanes(index)], sems.at[index, i])
            for i, (s, t) in enumerate(both)
        ]

    def pair_stores(index):
        both = zip((v_dq, v_dk, v_dv), (o_q, o_k, o_v))
        return [
            pltpu.make_async_copy(s.at[:, pair_lanes(index)], t.at[:, there(index)], sems.at[index, 5 + i])
            for i, (s, t) in enumerate(both)
        ]

    def slot_copy(index):
        slot = lax.rem(index, 2)
        return pltpu.make_async_copy(probs.at[pl.ds((first + index) * per, per)], slots.at[slot], slot_sems.at[slot])

    for copy in pair_loads(0):
        copy.start()
    slot_copy(0).start()
    for index in range(1, count):
        for copy in pair_loads(index):
            copy.start()

    def score_block(low, value, grad, column):
        return low.astype(f32) * (dot(value, grad, NT) - column)

    def body(index, carry):
        @pl.when(index + 1 < count)
        def _():
            slot_copy(index + 1).start()

        lanes = pair_lanes(index)
        slot = lax.rem(index, 2)
        for copy in pair_loads(index):
            copy.wait()
        key_block, value_block, query_block, grad_block = v_k[:, lanes], v_v[:, lanes], v_q[:, lanes], v_grad[:, lanes]
        inv_rows = inverse[pl.ds(first + index, 1)][0]
        inv_columns = jnp.concatenate([inv_rows, jnp.zeros((8 - per, inv_rows.shape[1]), f32)], axis=0).T
        scaled = grad_block.astype(f32) * sum(inv_columns[:, i : i + 1] * masks[i] for i in range(per))
        scaled = scaled.astype(bf16)
        product = scaled.astype(f32) * v_mix[:, lanes]
        columns = [jnp.sum(product * masks[i], axis=1, keepdims=True) for i in range(per)]
        wide_columns = sum(c * (lax.broadcasted_iota(jnp.int32, (1, 8), 1) == i).astype(f32) for i, c in enumerate(columns))
        column_rows = wide_columns.T
        slot_copy(index).wait()
        grads = [0.0, 0.0, 0.0]
        for i in range(per):
            column = column_rows[i : i + 1, :]
            grad = scaled * masks[i].astype(bf16)
            if fold:
                edge = grad.shape[0] // 2
                low, high = slice(0, edge), slice(edge, 2 * edge)
                cuts = ((low, low), (low, high), (high, high))
                probs_at = [slots[slot, i, k, q] for k, q in cuts]
                scores = [score_block(p, value_block[k], grad[q], column[:, q]) for p, (k, q) in zip(probs_at, cuts)]
                v_dist[index * per + i] = fold_diagonals(jnp.concatenate([scores[0] + scores[2], scores[1]], axis=1))
                lows = [x.astype(bf16) for x in scores]
                dq = [dot(lows[0], key_block[low], TN), dot(lows[1], key_block[low], TN) + dot(lows[2], key_block[high], TN)]
                dk = [dot(lows[0], query_block[low], NN) + dot(lows[1], query_block[high], NN), dot(lows[2], query_block[high], NN)]
                dv = [dot(probs_at[0], scaled[low], NN) + dot(probs_at[1], scaled[high], NN), dot(probs_at[2], scaled[high], NN)]
                terms_of = [jnp.concatenate(x, axis=0) for x in (dq, dk, dv)]
            else:
                probs_all = slots[slot, i]
                score_low = score_block(probs_all, value_block, grad, column).astype(bf16)
                terms_of = [dot(score_low, key_block, TN), dot(score_low, query_block, NN), dot(probs_all, scaled, NN)]
            grads = [g + x * masks[i] for g, x in zip(grads, terms_of)]
        v_dq[:, lanes] = grads[0].astype(bf16)
        v_dk[:, lanes] = grads[1].astype(bf16)
        v_dv[:, lanes] = grads[2].astype(bf16)
        for copy in pair_stores(index):
            copy.start()
        return carry

    lax.fori_loop(0, count, body, 0)
    if fold:
        dist_copy = pltpu.make_async_copy(v_dist, o_dist.at[pl.ds(first * per, count * per)], sems.at[0, 8])
        dist_copy.start()
        dist_copy.wait()
    for index in range(count):
        for copy in pair_stores(index):
            copy.wait()


def attend_back(order, head_size, fold, first, count, inverse, probs, exact_mix, grad_mixed, queries, keys, values, earlier=()):
    t, d = queries.shape
    e = keys.shape[0]
    per = LANES // head_size
    td, ed = (t, count * LANES), (e, count * LANES)
    out_shape = [shaped((t, d), bf16), shaped((e, d), bf16), shaped((e, d), bf16)]
    if fold:
        out_shape.append(shaped((d // head_size, 8, t), f32))
    scratch = [pltpu.VMEM(td, f32)] + [pltpu.VMEM(s, bf16) for s in (td, td, ed, ed, td, ed, ed)]
    scratch += [pltpu.VMEM((2, per, e, t), bf16), pltpu.SemaphoreType.DMA((count, 9)), pltpu.SemaphoreType.DMA((2,))]
    if fold:
        scratch.append(pltpu.VMEM((count * per, 8, t), f32))
    return order.call(
        partial(attend_back_kernel, head_size, fold, first, count, len(earlier)),
        out_shape=out_shape,
        in_specs=[VM] + [HBM] * (6 + len(earlier)),
        out_specs=[HBM] * len(out_shape),
        input_output_aliases={7 + i: i for i in range(len(earlier))},
        scratch_shapes=scratch,
        vmem=32,
        name="attend_back",
    )(inverse, probs, exact_mix, grad_mixed, queries, keys, values, *earlier)


def terms_kernel(count, place, *refs):
    lefts, rights, out = refs[:count], refs[count : 2 * count], refs[2 * count]
    v_lefts, v_rights, sent, sems = refs[2 * count + 1 : 3 * count + 1], refs[3 * count + 1 : 4 * count + 1], refs[-2], refs[-1]
    rows = out.shape[2]
    moves = Moves(sems)
    lanes = half_lanes(1 - place[0], 2 * rows)
    got = [(moves.load(lefts[u], v_lefts[u]), moves.load(rights[u].at[:, lanes], v_rights[u])) for u in range(count)]
    for u in range(count):
        here = pl.ds(u * rows, rows)
        for copy in got[u]:
            copy.wait()
        for b in range(2):
            sent[b, here, :] = dot(v_lefts[u][:, b * rows : (b + 1) * rows], v_rights[u][...], TN)
            moves.store(sent.at[b, here], out.at[b, here])
    moves.finish()


def terms(order, place, lefts, rights):
    count = len(lefts)
    d = lefts[0].shape[1]
    out = (2, count * (d // 2), d // 2)
    return order.call(
        partial(terms_kernel, count),
        out_shape=shaped(out, f32),
        in_specs=[SM] + [HBM] * (2 * count),
        out_specs=HBM,
        scratch_shapes=[pltpu.VMEM(x.shape, bf16) for x in lefts]
        + [pltpu.VMEM((x.shape[0], d // 2), bf16) for x in rights]
        + [pltpu.VMEM(out, f32), pltpu.SemaphoreType.DMA((4 * count,))],
        vmem=24,
        name="terms",
    )(place, *lefts, *rights)


def terms_kept_kernel(count, axes, place, *refs):
    lefts, rights = refs[:count], refs[count : 2 * count]
    sent, o_send, o_keep = refs[2 * count : 2 * count + 3]
    v_lefts, v_rights = refs[2 * count + 3 : 3 * count + 3], refs[3 * count + 3 : 4 * count + 3]
    v_sent, full, sems = refs[4 * count + 3 :]
    rows = sent.shape[2]
    moves = Moves(sems)
    lanes = half_lanes(place[0], 2 * rows)
    got = []
    for u in range(count):
        here = pl.ds(u * rows, rows)
        got.append(
            (
                moves.load(lefts[u], v_lefts[u]),
                moves.load(rights[u].at[:, lanes], v_rights[u]),
                moves.load(sent.at[:, here], v_sent.at[:, here]),
            )
        )
    for u in range(count):
        here = slice(u * rows, (u + 1) * rows)
        for copy in got[u]:
            copy.wait()
        for b in range(2):
            full[b, here, :] = v_sent[b, here, :] + dot(v_lefts[u][:, b * rows : (b + 1) * rows], v_rights[u][...], TN)
    cut_first(axes, place, full, o_send, o_keep)


def terms_kept(order, axes, place, lefts, rights, sent):
    count = len(lefts)
    d = lefts[0].shape[1]
    return order.call(
        partial(terms_kept_kernel, count, axes),
        out_shape=[shaped(sent.shape[1:], f32)] * 2,
        in_specs=[SM] + [HBM] * (2 * count) + [ANY],
        out_specs=[VM] * 2,
        scratch_shapes=[pltpu.VMEM(x.shape, bf16) for x in lefts]
        + [pltpu.VMEM((x.shape[0], d // 2), bf16) for x in rights]
        + [pltpu.VMEM(sent.shape, f32), pltpu.VMEM(sent.shape, f32), pltpu.SemaphoreType.DMA((3 * count,))],
        vmem=30,
        name="terms_kept",
    )(place, *lefts, *rights, sent)


def cross_close_kernel(
    rows, grad_two, stream1, dq, cq, wo, o_grad, o_low, o_mixed, o_gain,
    v_two, v_stream, v_dq, v_cq, v_wo, grad, low, mixed, sems,
):
    moves = Moves(sems)
    sources = (dq, cq, stream1, grad_two, wo)
    got = [moves.load(s, t) for s, t in zip(sources, (v_dq, v_cq, v_stream, v_two, v_wo))]
    for copy in got[:2]:
        copy.wait()
    back = dot(v_dq[...], v_cq[...], NT)
    for copy in got[2:4]:
        copy.wait()
    pulled, gain_grad = norm_pull(back, v_stream[...], rows[1:2, :])
    o_gain[...] = gain_grad
    grad[...] = v_two[...] + pulled
    moves.store(grad, o_grad)
    low[...] = grad[...].astype(bf16)
    moves.store(low, o_low)
    got[4].wait()
    mixed[...] = dot(low[...], v_wo[...], NT).astype(bf16)
    moves.store(mixed, o_mixed)
    moves.finish()


def cross_close(order, rows, grad_two, stream1, dq, cq, wo):
    t, d = dq.shape
    td, dd = (t, d), (d, d)
    return order.call(
        cross_close_kernel,
        out_shape=[shaped(td, f32), shaped(td, bf16), shaped(td, bf16), shaped((1, d), f32)],
        in_specs=[VM] + [HBM] * 5,
        out_specs=[HBM] * 3 + [VM],
        scratch_shapes=[pltpu.VMEM(td, f32), pltpu.VMEM(td, f32)]
        + [pltpu.VMEM(s, bf16) for s in (td, dd, dd)]
        + [pltpu.VMEM(td, f32), pltpu.VMEM(td, bf16), pltpu.VMEM(td, bf16)]
        + [pltpu.SemaphoreType.DMA((8,))],
        vmem=20,
        name="cross_close",
    )(rows, grad_two, stream1, dq, cq, wo)


def enc_close_kernel(dk, dv, ck, cv, out, v_dk, v_dv, v_ck, v_cv, total, sems):
    moves = Moves(sems)
    got = [moves.load(s, t) for s, t in ((dk, v_dk), (ck, v_ck), (dv, v_dv), (cv, v_cv))]
    for copy in got:
        copy.wait()
    rows = out.shape[0] // 2
    for i in range(2):
        here = pl.ds(i * rows, rows)
        total[here, :] = dot(v_dk[here, :], v_ck[...], NT) + dot(v_dv[here, :], v_cv[...], NT)
        moves.store(total.at[here], out.at[here])
    moves.finish()


def enc_close(order, dk, dv, ck, cv):
    e, d = dk.shape
    return order.call(
        enc_close_kernel,
        out_shape=shaped((e, d), f32),
        in_specs=[HBM] * 4,
        out_specs=HBM,
        scratch_shapes=[pltpu.VMEM((e, d), bf16)] * 2
        + [pltpu.VMEM((d, d), bf16)] * 2
        + [pltpu.VMEM((e, d), f32), pltpu.SemaphoreType.DMA((6,))],
        vmem=20,
        name="enc_close",
    )(dk, dv, ck, cv)


def self_close_kernel(
    table_shape, flag, rows, gain_b, gain_c, grad_one, dec, dq, dk, dv, dist, wq, wk, wv, o_grad, o_small,
    v_one, v_dec, v_dq, v_dk, v_dv, v_dist, v_wq, v_wk, v_wv, grad_zero, sems,
):
    t, d = dq.shape
    heads = dist.shape[0]
    num_buckets = table_shape[0]
    moves = Moves(sems)
    sources = (dq, wq, dk, wk, dv, wv, dec, grad_one, dist)
    targets = (v_dq, v_wq, v_dk, v_wk, v_dv, v_wv, v_dec, v_one, v_dist)
    got = [moves.load(s, t_) for s, t_ in zip(sources, targets)]
    dir_row = jnp.where(flag[0] == 0, rows[3:4, :], rows[4:5, :])
    back = None
    for i, (grad, weight) in enumerate(((v_dq, v_wq), (v_dk, v_wk), (v_dv, v_wv))):
        got[2 * i].wait()
        got[2 * i + 1].wait()
        term = dot(grad[...], weight[...], NT)
        back = term if back is None else back + term
    got[6].wait()
    got[7].wait()
    pulled, gain_grad = norm_pull(back, v_dec[...].astype(f32) + dir_row, rows[0:1, :])
    grad_zero[...] = v_one[...] + pulled
    moves.store(grad_zero, o_grad)
    row_sum = jnp.sum(grad_zero[...], axis=0, keepdims=True)
    picked = (flag[0] == 0).astype(f32)
    o_small[...] = jnp.zeros(o_small.shape, f32)
    o_small[0:1, :] = gain_grad
    o_small[1:2, :] = gain_b[...]
    o_small[2:3, :] = gain_c[...]
    o_small[3:4, :] = row_sum * picked
    o_small[4:5, :] = row_sum * (1.0 - picked)
    pick = lax.broadcasted_iota(jnp.int32, (num_buckets, t), 0).astype(f32) == rows[5:6, :t]
    got[8].wait()
    per_head = [jnp.sum(v_dist[h], axis=0, keepdims=True) for h in range(heads)]
    per_head += [jnp.zeros((1, t), f32)] * (-heads % 8)
    table = lax.dot_general(
        jnp.where(pick, 1.0, 0.0).astype(f32),
        jnp.concatenate(per_head, axis=0),
        NT,
        precision=lax.Precision.HIGHEST,
        preferred_element_type=f32,
    )
    o_small[8:, 0 : table.shape[1]] = table
    moves.finish()


def self_close(order, table_shape, flag, rows, gain_b, gain_c, grad_one, dec, dq, dk, dv, dist, wq, wk, wv):
    t, d = dq.shape
    td, dd = (t, d), (d, d)
    return order.call(
        partial(self_close_kernel, table_shape),
        out_shape=[shaped(td, f32), shaped((8 + table_shape[0], d), f32)],
        in_specs=[SM, VM, VM, VM] + [HBM] * 9,
        out_specs=[HBM, VM],
        scratch_shapes=[pltpu.VMEM(td, f32)]
        + [pltpu.VMEM(td, bf16)] * 4
        + [pltpu.VMEM(dist.shape, f32)]
        + [pltpu.VMEM(dd, bf16)] * 3
        + [pltpu.VMEM(td, f32), pltpu.SemaphoreType.DMA((10,))],
        vmem=24,
        name="self_close",
    )(flag, rows, gain_b, gain_c, grad_one, dec, dq, dk, dv, dist, wq, wk, wv)


class Links:
    def __init__(self, dp, rep):
        self.dp, self.rep = dp, rep
        self.lines = dp // 4

    def send(self, value, target):
        pairs = []
        for i in range(self.dp):
            for r in range(self.rep):
                line, side, core, to_rep = target(i // 4, i // 2 % 2, i % 2, r)
                pairs.append((i * self.rep + r, ((line * 2 + side) * 2 + core) * self.rep + to_rep))
        return lax.ppermute(value, ("dp", "rep"), pairs)

    def core(self, value):
        return self.send(value, lambda line, side, core, r: (line, side, core ^ 1, r))

    def line(self, value, flip):
        return self.send(value, lambda line, side, core, r: (line ^ flip, side, core, r))

    def swap(self, value, axes):
        def target(line, side, core, r):
            axis = axes[core]
            return line ^ (axis == "z"), side ^ (axis == "x"), core, r ^ (axis == "y")

        return self.send(value, target)

    def line_flips(self, first):
        flips = []
        while first < self.lines:
            flips.append(first)
            first *= 2
        return flips


def mebibytes(*arrays):
    return 2 + sum(-(-math.prod(a.shape) * 4 // 2**20) for a in arrays)


def add(order, a, b):
    def kernel(left, right, out):
        out[...] = left[...] + right[...]

    return order.call(
        kernel,
        in_specs=[VM, VM],
        out_specs=VM,
        out_shape=shaped(a.shape, f32),
        vmem=mebibytes(a, b, a),
        name="add",
    )(a, b)


def split_add(order, axes, place, keep, got):
    keep, got = (x.reshape((2, -1, x.shape[-1])) for x in (keep, got))

    def kernel(at, left, right, o_send, o_mine):
        mine = bit_of(at, axes)
        o_send[...] = left[1 - mine] + right[1 - mine]
        o_mine[...] = left[mine] + right[mine]

    return order.call(
        kernel,
        in_specs=[SM, VM, VM],
        out_specs=[VM, VM],
        out_shape=[shaped(keep.shape[1:], f32)] * 2,
        vmem=mebibytes(keep, got, keep),
        name="split_add",
    )(place, keep, got)


def join(order, axes, place, mine, far):
    def kernel(at, left, right, out):
        bit = bit_of(at, axes)
        out[bit] = left[...]
        out[1 - bit] = right[...]

    out = order.call(
        kernel,
        in_specs=[SM, VM, VM],
        out_specs=VM,
        out_shape=shaped((2,) + mine.shape, f32),
        vmem=mebibytes(mine, far, mine, far),
        name="join",
    )(place, mine, far)
    return out.reshape((-1, mine.shape[-1]))


def sum_bundle(order, links, place, ways, send, keep):
    steps = list(zip(*ways))
    back = list(zip(*([axis for axis in reversed(way) if axis != "y"] for way in ways)))
    got = links.swap(send, steps[0])
    yield
    for axes in steps[1:]:
        send, keep = split_add(order, axes, place, keep, got)
        got = links.swap(send, axes)
        yield
    mine = add(order, keep, got)
    for flip in links.line_flips(2):
        got = links.line(mine, flip)
        yield
        mine = add(order, mine, got)
    for axes in back:
        got = links.swap(mine, axes)
        yield
        mine = join(order, axes, place, mine, got)
    got = links.core(mine)
    yield
    return mine, got


def place_kernel(segments, aliased, place, mine, other, *refs):
    outs, sems = refs[aliased:-1], refs[-1]
    copies = []
    for i, (piece, core) in enumerate(((mine, place[0]), (other, 1 - place[0]))):
        for j, (first, count, out, row, base, step) in enumerate(segments):
            lanes = pl.ds(pl.multiple_of(base + core * step, LANES), piece.shape[1])
            copies.append(
                pltpu.make_async_copy(piece.at[pl.ds(first, count)], outs[out].at[pl.ds(row, count), lanes], sems.at[i, j])
            )
    for copy in copies:
        copy.start()
    for copy in copies:
        copy.wait()


def place_pieces(order, place, pieces, segments, out_shapes, aliased=()):
    return order.call(
        partial(place_kernel, segments, len(aliased)),
        in_specs=[SM, VM, VM] + [HBM] * len(aliased),
        out_specs=[HBM] * len(out_shapes),
        out_shape=out_shapes,
        input_output_aliases={3 + i: i for i in range(len(aliased))},
        scratch_shapes=[pltpu.SemaphoreType.DMA((2, len(segments)))],
        vmem=mebibytes(*pieces[:2]),
        name="place",
    )(place, *pieces, *aliased)


def sum_small(order, links, small):
    for axes in ("yy", "xx", "zz"):
        got = links.swap(small, axes)
        yield
        small = add(order, small, got)
    for flip in links.line_flips(2):
        got = links.line(small, flip)
        yield
        small = add(order, small, got)
    got = links.core(small)
    yield
    return add(order, small, got)


class Live:
    def __init__(self, steps):
        self.steps, self.result = steps, None
        self.step()

    def step(self):
        if self.result is None:
            try:
                next(self.steps)
            except StopIteration as end:
                self.result = end.value

    def finish(self):
        while self.result is None:
            self.step()
        return self.result


PLAN = (
    "fwd", "feed0", "feed1", "kept0", "result", "kept1", "close", "attb0", "F0", "attb1", "cterm0", "F1", "enc", "F0",
    "ckept0", "cclose", "F1", "F0", "atta0", "oterm0", "C0", "F1", "oterm1", "okept0", "F0", "okept1", "C0", "O0",
    "F0", "F1", "C0", "O1", "F1", "O0", "F0", "C0", "F0p", "O0", "O1", "sclose", "C0", "S", "O0", "F1", "O1", "O0",
    "F1p", "O1", "C0", "S", "O1", "S", "C0p", "S", "O0", "S", "O0p", "O1", "O1p",
)
FEED_CUTS = (2, 2)
FEED_WAYS = (("yxz", "xyz"), ("yxz", "xyz"))
CROSS_WAYS = (("yxz", "xyz"),)
OWN_WAYS = (("yxz", "xyz"), ("yxz", "yxz"))
ATTEND = (2, 1)


def local(
    dp, rep,
    dec_input, enc_states, out_cotangent, dec_lengths, group_ids, direction_flags, rel_buckets, step_index,
    self_gain, self_query, self_key, self_value, self_output, bucket_bias_table,
    cross_gain, cross_query, cross_key, cross_value, cross_output, feed_gain, feed_inner, feed_outer, dir_table,
):
    dec, enc, cot = dec_input[0], enc_states[0], out_cotangent[0]
    num_buckets, num_heads = bucket_bias_table.shape
    d = dec.shape[1]
    half = d // 2
    head_size = d // num_heads
    pairs = d // LANES
    links = Links(dp, rep)
    dp_index, rep_index = lax.axis_index("dp"), lax.axis_index("rep")
    place = jnp.stack([dp_index % 2, rep_index, (dp_index // 4) % 2, (dp_index // 2) % 2]).astype(jnp.int32)
    phase = full_turn * step_index.astype(f32) / PERIOD
    weight = 1.0 + 0.5 * jnp.cos(phase + full_turn * group_ids.astype(f32) / 3.0)
    length, flag = dec_lengths, direction_flags
    order = Order()
    env = {}
    live = {}
    block = feed_inner.shape[1] // 2
    starts = [sum(FEED_CUTS[:i]) for i in range(len(FEED_CUTS))]
    cuts = tuple((a * half, n * half) for a, n in zip(starts, FEED_CUTS))
    actives, pulls, sents = {}, {}, {}
    outer_shape = shaped((feed_outer.shape[0] // rep, d), f32)
    inner_shape = shaped((d // rep, feed_inner.shape[1]), f32)
    feed_grads = []
    done = {}

    def run_forward():
        names = (
            "input_a", "q", "k", "v", "mixed_a", "stream1", "input_b", "xq", "ek", "ev", "mixed_b", "stream2", "input_c",
            "probs_a", "probs_b", "exact_a", "exact_b", "rows", "inv_a", "inv_b",
        )
        smalls = (self_gain, cross_gain, feed_gain, dir_table, rel_buckets, bucket_bias_table.T)
        weights = (self_query, self_key, self_value, self_output, cross_query, cross_key, cross_value, cross_output)
        env.update(zip(names, forward(order, head_size, num_buckets, flag, smalls, dec, enc, weights)))

    def run_feed(p):
        actives[p], pulls[p], sent = feed(order, *cuts[p], place, weight, length, cot, env["input_c"], feed_inner, feed_outer)
        sents[p] = links.core(sent)

    def run_kept(p):
        first = [way[0] for way in FEED_WAYS[p]]
        send, keep = feed_kept(order, first, place, weight, length, cot, env["input_c"], actives[p], pulls[p], sents[p])
        live[f"F{p}"] = Live(sum_bundle(order, links, place, FEED_WAYS[p], send, keep))

    def run_close():
        pulled = [pulls[i] for i in range(len(cuts))]
        outs = close(order, cuts, weight, length, env["rows"], cot, env["stream2"], pulled, feed_inner, cross_output)
        env.update(zip(("grad_two", "low_two", "grad_mixed_b", "gain_c_grad"), outs))

    def run_result():
        active = [actives[i] for i in range(len(cuts))]
        env["block_output"] = block_result(order, cuts, length, env["stream2"], active, feed_outer)

    def run_attend(i, groups, fold, name, *args):
        count = pairs // groups
        env[name] = attend_back(order, head_size, fold, i * count, count, *(env[a] for a in args), earlier=env.get(name, ()))

    def run_cross_close():
        outs = cross_close(
            order, env["rows"], env["grad_two"], env["stream1"], env["back_b"][0], cross_query, self_output
        )
        env.update(zip(("grad_one", "low_one", "grad_mixed_a", "gain_b_grad"), outs))

    def run_enc_close():
        env["enc_grad"] = enc_close(order, *env["back_b"][1:], cross_key, cross_value)

    def run_self_close():
        outs = self_close(
            order, bucket_bias_table.shape, flag, env["rows"], env["gain_b_grad"], env["gain_c_grad"], env["grad_one"], dec,
            *env["back_a"], self_query, self_key, self_value,
        )
        env["input_grad"], small = outs
        live["S"] = Live(sum_small(order, links, small))

    def operands(own):
        if own:
            dq, dk, dv, _ = env["back_a"]
            return (env["mixed_a"], env["input_a"], env["input_a"], env["input_a"]), (env["low_one"], dq, dk, dv)
        dq, dk, dv = env["back_b"]
        return (env["mixed_b"], env["input_b"], enc, enc), (env["low_two"], dq, dk, dv)

    def piece(own, i):
        count = 4 // len(OWN_WAYS if own else CROSS_WAYS)
        return [x[i * count : (i + 1) * count] for x in operands(own)]

    def run_terms(own, i):
        sents[own, i] = links.core(terms(order, place, *piece(own, i)))

    def run_terms_kept(own, i):
        ways = (OWN_WAYS if own else CROSS_WAYS)[i]
        send, keep = terms_kept(order, [way[0] for way in ways], place, *piece(own, i), sents[own, i])
        live[f"{'O' if own else 'C'}{i}"] = Live(sum_bundle(order, links, place, ways, send, keep))

    def run_place(name):
        pieces = live[name].finish()
        if name[0] == "F":
            offset, split = cuts[int(name[1:])]
            segments = [(0, split, 0, offset, 0, half)]
            segments += [(split + i * half, half, 1, 0, offset + i * half, block) for i in range(split // half)]
            feed_grads[:] = place_pieces(order, place, pieces, segments, [outer_shape, inner_shape], feed_grads)
        else:
            count = 4 // len(OWN_WAYS if name[0] == "O" else CROSS_WAYS)
            segments = [(j * half, half, j, 0, 0, half) for j in range(count)]
            done[name] = place_pieces(order, place, pieces, segments, [shaped((half, d), f32)] * count)

    for name in PLAN:
        head = name.rstrip("0123456789p")
        index = int(name[len(head)]) if name[-1].isdigit() else None
        if name == "fwd":
            run_forward()
        elif head == "feed":
            run_feed(index)
        elif head == "kept":
            run_kept(index)
        elif name == "close":
            run_close()
        elif name == "result":
            run_result()
        elif name == "enc":
            run_enc_close()
        elif head == "attb":
            run_attend(index, ATTEND[0], False, "back_b", "inv_b", "probs_b", "exact_b", "grad_mixed_b", "xq", "ek", "ev")
        elif head == "atta":
            run_attend(index, ATTEND[1], True, "back_a", "inv_a", "probs_a", "exact_a", "grad_mixed_a", "q", "k", "v")
        elif name == "cclose":
            run_cross_close()
        elif name == "sclose":
            run_self_close()
        elif head in ("oterm", "cterm"):
            run_terms(head == "oterm", index)
        elif head in ("okept", "ckept"):
            run_terms_kept(head == "okept", index)
        elif name.endswith("p"):
            run_place(name[:-1])
        else:
            live[name].step()

    outer, inner = feed_grads
    small = live["S"].finish()
    cross = [x for i in range(len(CROSS_WAYS)) for x in done[f"C{i}"]]
    own = [x for i in range(len(OWN_WAYS)) for x in done[f"O{i}"]]
    small_rows = lambda i: lax.dynamic_slice_in_dim(small[i], rep_index * half, half)
    table_rows = num_buckets // rep
    table = lax.dynamic_slice(small, (8 + rep_index * table_rows, 0), (table_rows, num_heads))
    dir_grad = lax.dynamic_slice_in_dim(small, 3 + rep_index, 1)
    return (
        env["block_output"][None],
        env["input_grad"][None],
        env["enc_grad"][None],
        small_rows(0),
        own[1],
        own[2],
        own[3],
        own[0],
        table,
        small_rows(1),
        cross[1],
        cross[2],
        cross[3],
        cross[0],
        small_rows(2),
        inner,
        outer,
        dir_grad,
    )


def solution(mesh):
    pair = P(("dp", "rep"), None, None)
    each = P(("dp", "rep"))
    rows = P("rep", None)
    vector = P("rep")
    return jax.shard_map(
        partial(local, mesh.shape["dp"], mesh.shape["rep"]),
        mesh=mesh,
        in_specs=(pair, pair, pair, each, each, each) + (P(),) * 17,
        out_specs=(
            pair, pair, pair, vector, rows, rows, rows, rows, rows, vector, rows, rows, rows, rows, vector, rows, rows, rows,
        ),
        check_vma=False,
    )
```

```python
from functools import partial
import math

import jax
import jax.numpy as jnp
from jax import lax
from jax.experimental import pallas as pl
from jax.experimental.pallas import tpu as pltpu
from jax.sharding import PartitionSpec as P

PERIOD = 1000
full_turn = 2.0 * math.pi
norm_eps = 1e-06
masked_score = -1e30
LANES = 128
FLOPS = 2 * 10**10
BYTES = 10**7
f32 = jnp.float32
bf16 = jnp.bfloat16

NN = (((1,), (0,)), ((), ()))
NT = (((1,), (1,)), ((), ()))
TN = (((0,), (0,)), ((), ()))


def dot(left, right, form):
    return lax.dot_general(left, right, form, preferred_element_type=f32)


def shaped(shape, dtype):
    return jax.ShapeDtypeStruct(shape, dtype)


class Order:
    def __init__(self):
        self.last, self.held = None, False

    def call(self, kernel, *, in_specs, out_shape, out_specs, vmem, **more):
        count = len(in_specs)
        held = lambda shape, spec: pltpu.HBM(shape.shape, shape.dtype) if spec is HBM else shape
        if isinstance(out_specs, list):
            out_shape = [held(a, b) for a, b in zip(out_shape, out_specs)]
        else:
            out_shape = held(out_shape, out_specs)

        def apply(*args):
            after = [] if self.last is None or any(self.last is a for a in args) else [self.last]
            if self.held:
                after = [pltpu.with_memory_space_constraint(a, pltpu.HBM) for a in after]

            def ordered(*refs):
                return kernel(*refs[:count], *refs[count + len(after) :])

            args = [
                pltpu.with_memory_space_constraint(a, pltpu.HBM) if s is HBM or s is FROM_HBM else a
                for a, s in zip(args, in_specs)
            ]
            outs = pl.pallas_call(
                ordered,
                in_specs=list(in_specs) + [ANY] * len(after),
                out_shape=out_shape,
                out_specs=out_specs,
                compiler_params=pltpu.CompilerParams(vmem_limit_bytes=vmem * 2**20),
                cost_estimate=pl.CostEstimate(flops=FLOPS, bytes_accessed=BYTES, transcendentals=0),
                **more,
            )(*args, *after)
            self.last, self.held = jax.tree.leaves(outs)[0], jax.tree.leaves(out_specs)[0] is HBM
            return outs

        return apply


HBM = pl.BlockSpec(memory_space=pltpu.HBM)
ANY = pl.BlockSpec(memory_space=pl.ANY)
VM = pl.BlockSpec(memory_space=pltpu.VMEM)
FROM_HBM = pl.BlockSpec(memory_space=pltpu.VMEM)
SM = pl.BlockSpec(memory_space=pltpu.SMEM)
AXES = {"y": 1, "z": 2, "x": 3}


class Moves:
    def __init__(self, sems):
        self.sems, self.count, self.stores = sems, 0, []

    def load(self, source, target):
        copy = pltpu.make_async_copy(source, target, self.sems.at[self.count])
        self.count += 1
        copy.start()
        return copy

    def store(self, source, target):
        self.stores.append(self.load(source, target))

    def finish(self):
        for copy in self.stores:
            copy.wait()


def norm_rows(stream, gain):
    scale = lax.rsqrt(jnp.mean(stream * stream, axis=-1, keepdims=True) + norm_eps)
    return stream * scale * gain


def norm_pull(grad_out, stream, gain):
    scale = lax.rsqrt(jnp.mean(stream * stream, axis=-1, keepdims=True) + norm_eps)
    normed = stream * scale
    gain_grad = jnp.sum(grad_out * normed, axis=0, keepdims=True)
    grad_normed = grad_out * gain
    inner_mean = jnp.mean(grad_normed * normed, axis=-1, keepdims=True)
    return scale * (grad_normed - normed * inner_mean), gain_grad


def weighted(cot, length, weight):
    valid = (lax.broadcasted_iota(jnp.int32, (cot.shape[0], 1), 0) < length[0]).astype(f32)
    return valid, valid * (cot[...].astype(f32) * weight[0])


def head_masks(width, head_size):
    lane = lax.broadcasted_iota(jnp.int32, (1, width), 1)
    return [jnp.where(lane // head_size == i, 1.0, 0.0).astype(f32) for i in range(width // head_size)]


def pair_lanes(index):
    return pl.ds(pl.multiple_of(index * LANES, LANES), LANES)


def half_lanes(half, width):
    return pl.ds(pl.multiple_of(half * (width // 2), LANES), width // 2)


def forward_kernel(
    head_size, num_buckets,
    flag, self_gain, cross_gain, feed_gain, dirs, buckets, table, dec, enc, wq, wk, wv, wo, cq, ck, cv, co,
    o_input_a, o_q, o_k, o_v, o_mixed_a, o_stream1, o_input_b, o_cq, o_ek, o_ev, o_mixed_b, o_stream2, o_input_c,
    o_pa, o_pb, o_exact_a, o_exact_b, rows, o_inv_a, o_inv_b,
    v_dec, v_enc, v_wq, v_wk, v_wv, v_wo, v_cq, v_ck, v_cv, v_co,
    input_a, q, k, v, mixed_a, stream1, input_b, xq, ek, ev, mixed_b, stream2, input_c,
    exact_a, exact_b, dist, slots_a, slots_b, sems, slot_sems,
):
    dec_len, width = dec.shape
    pairs = width // LANES
    per = LANES // head_size
    moves = Moves(sems)
    names = (v_dec, v_wq, v_wk, v_wv, v_enc, v_ck, v_cv, v_wo, v_cq, v_co)
    loads = [moves.load(s, t) for s, t in zip((dec, wq, wk, wv, enc, ck, cv, wo, cq, co), names)]
    flat = lambda ref: ref[...].astype(f32).reshape(1, ref.shape[0])
    gain_a, gain_b, gain_c = flat(self_gain), flat(cross_gain), flat(feed_gain)
    rows[...] = jnp.zeros(rows.shape, f32)
    for i, row in enumerate((gain_a, gain_b, gain_c)):
        rows[i : i + 1, :] = row
    rows[3:5, :] = dirs[...].astype(f32)
    rows[5:6, 0:dec_len] = flat(buckets)
    pick = lax.broadcasted_iota(jnp.int32, (num_buckets, dec_len), 0).astype(f32) == rows[5:6, :dec_len]
    dist[0 : table.shape[0], :] = dot(table[...], jnp.where(pick, 1.0, 0.0).astype(bf16), NN)
    dir_row = jnp.where(flag[0] == 0, rows[3:4, :], rows[4:5, :])
    loads[0].wait()
    input_a[...] = norm_rows(v_dec[...].astype(f32) + dir_row, gain_a).astype(bf16)
    moves.store(input_a, o_input_a)
    for load, weight, target, out in ((1, v_wq, q, o_q), (2, v_wk, k, o_k), (3, v_wv, v, o_v)):
        loads[load].wait()
        target[...] = dot(input_a[...], weight[...], NN).astype(bf16)
        moves.store(target, out)
    loads[4].wait()
    for load, weight, target, out in ((5, v_ck, ek, o_ek), (6, v_cv, ev, o_ev)):
        loads[load].wait()
        target[...] = dot(v_enc[...], weight[...], NN).astype(bf16)
        moves.store(target, out)
    masks = head_masks(LANES, head_size)
    edge = dec_len // 2
    key_pos = lax.broadcasted_iota(jnp.int32, (edge, edge), 0)
    query_pos = lax.broadcasted_iota(jnp.int32, (edge, edge), 1)

    def attend(queries, keys, values, mixed, exact_mix, slots, out, inverse, head_rows):
        def slot_copy(index, slot):
            return pltpu.make_async_copy(slots.at[slot], out.at[pl.ds(index * per, per)], slot_sems.at[slot])

        def sweep(by_top):
            def body(index, bounds):
                slot = lax.rem(index, 2)

                @pl.when(index >= 2)
                def _():
                    slot_copy(index - 2, slot).wait()

                lanes = pair_lanes(index)
                key_block, value_rows, query_block = keys[:, lanes], values[:, lanes].T, queries[:, lanes]
                ones = jnp.ones((16, value_rows.shape[1]), bf16)
                parts, sums = [], []
                least, most = bounds
                for i in range(per):
                    mix = jnp.concatenate([value_rows[i * head_size : (i + 1) * head_size], ones], axis=0)
                    total = head_rows(by_top, index, i, slot, key_block, query_block * masks[i].astype(bf16), mix)
                    norm = total[head_size : head_size + 1, :]
                    least, most = jnp.minimum(least, norm), jnp.maximum(most, norm)
                    inv = 1.0 / norm
                    parts.append(total[0:head_size, :] * inv)
                    sums.append(inv)
                both = jnp.concatenate(parts, axis=0).T
                exact_mix[:, lanes] = both
                mixed[:, lanes] = both.astype(bf16)
                inverse[pl.ds(index, 1)] = jnp.concatenate(sums, axis=0)[None]
                slot_copy(index, slot).start()
                return least, most

            bounds = lax.fori_loop(0, pairs, body, (jnp.ones((1, dec_len), f32), jnp.ones((1, dec_len), f32)))
            for index in range(max(pairs - 2, 0), pairs):
                slot_copy(index, index % 2).wait()
            return bounds

        least, most = sweep(False)
        safe = jnp.logical_and(jnp.min(least) > 1e-15, jnp.max(most) < 1e15)

        @pl.when(jnp.logical_not(safe))
        def _():
            sweep(True)

    def raised(scores, top):
        return jnp.exp(scores if top is None else scores - top).astype(bf16)

    def top_of(by_top, *blocks):
        if not by_top:
            return None
        tops = [jnp.max(x, axis=0, keepdims=True) for x in blocks]
        return tops[0] if len(tops) == 1 else jnp.maximum(*tops)

    def own_rows(by_top, index, i, slot, key_block, query, mix):
        row = dist[pl.ds(index * per + i, 1), :]
        bias = pltpu.roll(jnp.broadcast_to(row, (edge, dec_len)), 0, 1, stride=1, stride_axis=0)
        seen = key_pos <= query_pos
        low, high = slice(0, edge), slice(edge, dec_len)
        near = jnp.where(seen, dot(key_block[low], query[low], NT) + bias[:, low], masked_score)
        first = raised(near, top_of(by_top, near))
        slots_a[slot, i, low, low] = first
        far = dot(key_block[low], query[high], NT) + bias[:, high]
        near = jnp.where(seen, dot(key_block[high], query[high], NT) + bias[:, low], masked_score)
        top = top_of(by_top, far, near)
        second, third = raised(far, top), raised(near, top)
        slots_a[slot, i, low, high] = second
        slots_a[slot, i, high, high] = third
        right = dot(mix[:, low], second, NN) + dot(mix[:, high], third, NN)
        return jnp.concatenate([dot(mix[:, low], first, NN), right], axis=1)

    def cross_rows(by_top, index, i, slot, key_block, query, mix):
        scores = dot(key_block, query, NT)
        low = raised(scores, top_of(by_top, scores))
        slots_b[slot, i] = low
        return dot(mix, low, NN)

    attend(q, k, v, mixed_a, exact_a, slots_a, o_pa, o_inv_a, own_rows)
    moves.store(mixed_a, o_mixed_a)
    moves.store(exact_a, o_exact_a)
    loads[7].wait()
    stream1[...] = v_dec[...].astype(f32) + dir_row + dot(mixed_a[...], v_wo[...], NN)
    moves.store(stream1, o_stream1)
    input_b[...] = norm_rows(stream1[...], gain_b).astype(bf16)
    moves.store(input_b, o_input_b)
    loads[8].wait()
    xq[...] = dot(input_b[...], v_cq[...], NN).astype(bf16)
    moves.store(xq, o_cq)
    attend(xq, ek, ev, mixed_b, exact_b, slots_b, o_pb, o_inv_b, cross_rows)
    moves.store(mixed_b, o_mixed_b)
    moves.store(exact_b, o_exact_b)
    loads[9].wait()
    stream2[...] = stream1[...] + dot(mixed_b[...], v_co[...], NN)
    moves.store(stream2, o_stream2)
    input_c[...] = norm_rows(stream2[...], gain_c).astype(bf16)
    moves.store(input_c, o_input_c)
    moves.finish()


def forward(order, head_size, num_buckets, flag, smalls, dec, enc, weights):
    t, d = dec.shape
    e = enc.shape[0]
    heads = d // head_size
    per = LANES // head_size
    td, ed = (t, d), (e, d)
    low = [td, td, td, td, td, None, td, td, ed, ed, td, None, td]
    outs = [shaped(s, bf16) if s else shaped(td, f32) for s in low]
    outs += [shaped((heads, t, t), bf16), shaped((heads, e, t), bf16), shaped(td, f32), shaped(td, f32)]
    outs += [shaped((8, d), f32)]
    outs += [shaped((heads // per, per, t), f32)] * 2
    scratch = [pltpu.VMEM(td, bf16), pltpu.VMEM(ed, bf16)] + [pltpu.VMEM((d, d), bf16)] * 8
    scratch += [pltpu.VMEM(s, bf16) if s else pltpu.VMEM(td, f32) for s in low]
    scratch += [
        pltpu.VMEM(td, f32),
        pltpu.VMEM(td, f32),
        pltpu.VMEM((-(-heads // 8) * 8, t), f32),
        pltpu.VMEM((2, per, t, t), bf16),
        pltpu.VMEM((2, per, e, t), bf16),
        pltpu.SemaphoreType.DMA((25,)),
        pltpu.SemaphoreType.DMA((2,)),
    ]
    return order.call(
        partial(forward_kernel, head_size, num_buckets),
        out_shape=outs,
        in_specs=[SM] + [FROM_HBM] * 6 + [HBM] * 10,
        out_specs=[HBM] * (len(outs) - 3) + [VM] * 3,
        scratch_shapes=scratch,
        vmem=52,
        name="forward",
    )(flag, *smalls, dec, enc, *weights)


def feed_kernel(
    offset, place, weight, length, cot, input_c, w1, w2, o_active, o_pull, o_sent,
    v_cot, v_input, v_w1, v_w2, grad_low, active, pull, sent, sems,
):
    d = cot.shape[1]
    split = v_w1.shape[2]
    block = w1.shape[1] // 2
    rows = d // 2
    moves = Moves(sems)
    columns = [pl.ds(b * block + offset, split) for b in range(2)]
    got_input = moves.load(input_c, v_input)
    got = [[moves.load(w1.at[:, columns[0]], v_w1.at[0])], []]
    got_cot = moves.load(cot, v_cot)
    got[0].append(moves.load(w2.at[columns[0], :], v_w2.at[0]))
    got[1] += [moves.load(w1.at[:, columns[1]], v_w1.at[1]), moves.load(w2.at[columns[1], :], v_w2.at[1])]
    other = 1 - place[0]
    lanes = half_lanes(other, d)
    got_input.wait()
    for b in range(2):
        got[b][0].wait()
        inner = dot(v_input[...], v_w1[b], NN)
        if b == 0:
            got_cot.wait()
            grad_low[...] = weighted(v_cot, length, weight)[1].astype(bf16)
        got[b][1].wait()
        back = dot(grad_low[...], v_w2[b], NT)
        root = math.sqrt(2.0 / math.pi)
        square = inner * inner
        bent = jnp.tanh(root * (inner + 0.044715 * (square * inner)))
        half_up = 0.5 * (1.0 + bent)
        slope = half_up + (0.5 * inner) * (1.0 - bent * bent) * (root * (1.0 + 3.0 * 0.044715 * square))
        active[b] = (inner * half_up).astype(bf16)
        moves.store(active.at[b], o_active.at[b])
        pull[b] = (back * slope).astype(bf16)
        moves.store(pull.at[b], o_pull.at[b])
    for b in range(2):
        sent[b, 0:split, :] = dot(active[b], grad_low[:, lanes], TN)
        for i in range(split // rows):
            sent[b, split + i * rows : split + (i + 1) * rows, :] = dot(
                v_input[:, b * rows : (b + 1) * rows], pull[other, :, i * rows : (i + 1) * rows], TN
            )
        moves.store(sent.at[b], o_sent.at[b])
    moves.finish()


def feed(order, offset, split, place, weight, length, cot, input_c, w1, w2):
    t, d = cot.shape
    wide = (2, t, split)
    out = (2, 2 * split, d // 2)
    return order.call(
        partial(feed_kernel, offset),
        out_shape=[shaped(wide, bf16), shaped(wide, bf16), shaped(out, f32)],
        in_specs=[SM, SM, SM, HBM, HBM, HBM, HBM],
        out_specs=[HBM] * 3,
        scratch_shapes=[
            pltpu.VMEM((t, d), bf16),
            pltpu.VMEM((t, d), bf16),
            pltpu.VMEM((2, d, split), bf16),
            pltpu.VMEM((2, split, d), bf16),
            pltpu.VMEM((t, d), bf16),
            pltpu.VMEM(wide, bf16),
            pltpu.VMEM(wide, bf16),
            pltpu.VMEM(out, f32),
            pltpu.SemaphoreType.DMA((12,)),
        ],
        vmem=32,
        name="feed",
    )(place, weight, length, cot, input_c, w1, w2)


def bit_of(place, axes):
    return jnp.where(place[0] == 0, place[AXES[axes[0]]], place[AXES[axes[1]]])


def cut_first(axes, place, full, out_send, out_keep):
    count = full.shape[1] // 2
    for core in range(2):

        @pl.when(place[0] == core)
        def _(core=core):
            bit = place[AXES[axes[core]]]
            for out, at in ((out_send, 1 - bit), (out_keep, bit)):
                if axes[core] == "y":
                    out[...] = full[at]
                else:
                    for b in range(2):
                        out[b * count : (b + 1) * count, :] = full[b, pl.ds(pl.multiple_of(at * count, 8), count), :]


def feed_kept_kernel(
    axes, place, weight, length, cot, input_c, active, pull, sent, o_send, o_keep,
    v_cot, v_input, v_active, v_pull, v_sent, grad_low, full, sems,
):
    d = cot.shape[1]
    split = active.shape[2]
    rows = d // 2
    half = place[0]
    moves = Moves(sems)
    lanes = half_lanes(half, d)
    got = [moves.load(cot.at[:, lanes], v_cot), moves.load(active, v_active), moves.load(sent, v_sent)]
    got += [moves.load(input_c, v_input), moves.load(pull.at[half], v_pull)]
    got[0].wait()
    grad_low[...] = weighted(v_cot, length, weight)[1].astype(bf16)
    got[1].wait()
    got[2].wait()
    for b in range(2):
        full[b, 0:split, :] = v_sent[b, 0:split, :] + dot(v_active[b], grad_low[...], TN)
    got[3].wait()
    got[4].wait()
    for b in range(2):
        for i in range(split // rows):
            here = slice(split + i * rows, split + (i + 1) * rows)
            full[b, here, :] = v_sent[b, here, :] + dot(
                v_input[:, b * rows : (b + 1) * rows], v_pull[:, i * rows : (i + 1) * rows], TN
            )
    cut_first(axes, place, full, o_send, o_keep)


def feed_kept(order, axes, place, weight, length, cot, input_c, active, pull, sent):
    t, d = cot.shape
    split = active.shape[2]
    return order.call(
        partial(feed_kept_kernel, axes),
        out_shape=[shaped(sent.shape[1:], f32)] * 2,
        in_specs=[SM, SM, SM] + [HBM] * 4 + [ANY],
        out_specs=[VM] * 2,
        scratch_shapes=[
            pltpu.VMEM((t, d // 2), bf16),
            pltpu.VMEM((t, d), bf16),
            pltpu.VMEM((2, t, split), bf16),
            pltpu.VMEM((t, split), bf16),
            pltpu.VMEM(sent.shape, f32),
            pltpu.VMEM((t, d // 2), bf16),
            pltpu.VMEM(sent.shape, f32),
            pltpu.SemaphoreType.DMA((5,)),
        ],
        vmem=30,
        name="feed_kept",
    )(place, weight, length, cot, input_c, active, pull, sent)


def close_kernel(cuts, *refs):
    parts = len(cuts)
    weight, length, rows, cot, stream2 = refs[:5]
    pulls = refs[5 : 5 + parts]
    w1, wo, o_grad, o_low, o_mixed, o_gain, v_cot, v_stream, v_pull, v_w1, v_wo, grad, low, mixed, sems = refs[5 + parts :]
    block = w1.shape[1] // 2
    moves = Moves(sems)
    got = []
    for b in range(2):
        for p, (offset, split) in enumerate(cuts):
            here = pl.ds(b * block + offset, split)
            got.append(moves.load(pulls[p].at[b], v_pull.at[:, here]))
            got.append(moves.load(w1.at[:, here], v_w1.at[:, here]))
    got_stream, got_cot = moves.load(stream2, v_stream), moves.load(cot, v_cot)
    got_wo = moves.load(wo, v_wo)
    back = None
    for b in range(2):
        here = slice(b * block, (b + 1) * block)
        for copy in got[b * 2 * parts : (b + 1) * 2 * parts]:
            copy.wait()
        term = dot(v_pull[:, here], v_w1[:, here], NT)
        back = term if back is None else back + term
    got_stream.wait()
    pulled, gain_grad = norm_pull(back, v_stream[...], rows[2:3, :])
    o_gain[...] = gain_grad
    got_cot.wait()
    grad[...] = pulled + weighted(v_cot, length, weight)[1]
    moves.store(grad, o_grad)
    low[...] = grad[...].astype(bf16)
    moves.store(low, o_low)
    got_wo.wait()
    mixed[...] = dot(low[...], v_wo[...], NT).astype(bf16)
    moves.store(mixed, o_mixed)
    moves.finish()


def close(order, cuts, weight, length, rows, cot, stream2, pulls, w1, wo):
    t, d = cot.shape
    parts = len(cuts)
    td = (t, d)
    return order.call(
        partial(close_kernel, cuts),
        out_shape=[shaped(td, f32), shaped(td, bf16), shaped(td, bf16), shaped((1, d), f32)],
        in_specs=[SM, SM, VM] + [HBM] * (4 + parts),
        out_specs=[HBM] * 3 + [VM],
        scratch_shapes=[
            pltpu.VMEM(td, bf16),
            pltpu.VMEM(td, f32),
            pltpu.VMEM((t, w1.shape[1]), bf16),
            pltpu.VMEM(w1.shape, bf16),
            pltpu.VMEM((d, d), bf16),
            pltpu.VMEM(td, f32),
            pltpu.VMEM(td, bf16),
            pltpu.VMEM(td, bf16),
            pltpu.SemaphoreType.DMA((4 * parts + 6,)),
        ],
        vmem=30,
        name="close",
    )(weight, length, rows, cot, stream2, *pulls, w1, wo)


def result_kernel(cuts, *refs):
    parts = len(cuts)
    length, stream2 = refs[:2]
    actives = refs[2 : 2 + parts]
    w2, out, v_stream, v_active, v_w2, sems = refs[2 + parts :]
    block = w2.shape[0] // 2
    moves = Moves(sems)
    got = []
    for b in range(2):
        for p, (offset, split) in enumerate(cuts):
            here = pl.ds(b * block + offset, split)
            got.append(moves.load(actives[p].at[b], v_active.at[:, here]))
            got.append(moves.load(w2.at[here, :], v_w2.at[here, :]))
    got.append(moves.load(stream2, v_stream))
    for copy in got:
        copy.wait()
    valid = (lax.broadcasted_iota(jnp.int32, (out.shape[0], 1), 0) < length[0]).astype(f32)
    out[...] = (valid * (v_stream[...] + dot(v_active[...], v_w2[...], NN))).astype(bf16)


def block_result(order, cuts, length, stream2, actives, w2):
    t, d = stream2.shape
    parts = len(cuts)
    return order.call(
        partial(result_kernel, cuts),
        out_shape=shaped((t, d), bf16),
        in_specs=[SM] + [HBM] * (2 + parts),
        out_specs=VM,
        scratch_shapes=[
            pltpu.VMEM((t, d), f32),
            pltpu.VMEM((t, w2.shape[0]), bf16),
            pltpu.VMEM(w2.shape, bf16),
            pltpu.SemaphoreType.DMA((4 * parts + 1,)),
        ],
        vmem=24,
        name="result",
    )(length, stream2, *actives, w2)


def fold_diagonals(tiles):
    count, length = tiles.shape
    steps = LANES // 8
    total = None
    for u in range(steps):
        acc = None
        for k in range(count // LANES):
            t = k * steps + u
            tile = tiles[8 * t : 8 * t + 8, :]
            if k:
                tile = jnp.concatenate([tile[:, LANES * k :], tile[:, : LANES * k]], axis=1)
            acc = tile if acc is None else acc + tile
        if u:
            acc = pltpu.roll(acc, length - 8 * u, 1)
        total = acc if total is None else total + acc
    rows = lax.broadcasted_iota(jnp.int32, (8, length), 0)
    for b in (1, 2, 4):
        total = jnp.where((rows & b) != 0, pltpu.roll(total, length - b, 1), total)
    return total


def attend_back_kernel(
    head_size, fold, first, count, earlier, inverse, probs, exact_mix, grad_mixed, queries, keys, values, *refs
):
    refs = refs[earlier:]
    o_q, o_k, o_v = refs[:3]
    o_dist = refs[3] if fold else None
    v_mix, v_grad, v_q, v_k, v_v, v_dq, v_dk, v_dv, slots, sems, slot_sems = refs[3 + fold : 14 + fold]
    v_dist = refs[14 + fold] if fold else None
    per = LANES // head_size
    masks = head_masks(LANES, head_size)

    def there(index):
        return pl.ds(pl.multiple_of((first + index) * LANES, LANES), LANES)

    def pair_loads(index):
        both = zip((values, grad_mixed, exact_mix, keys, queries), (v_v, v_grad, v_mix, v_k, v_q))
        return [
            pltpu.make_async_copy(s.at[:, there(index)], t.at[:, pair_lanes(index)], sems.at[index, i])
            for i, (s, t) in enumerate(both)
        ]

    def pair_stores(index):
        both = zip((v_dq, v_dk, v_dv), (o_q, o_k, o_v))
        return [
            pltpu.make_async_copy(s.at[:, pair_lanes(index)], t.at[:, there(index)], sems.at[index, 5 + i])
            for i, (s, t) in enumerate(both)
        ]

    def slot_copy(index):
        slot = lax.rem(index, 2)
        return pltpu.make_async_copy(probs.at[pl.ds((first + index) * per, per)], slots.at[slot], slot_sems.at[slot])

    for copy in pair_loads(0):
        copy.start()
    slot_copy(0).start()
    for index in range(1, count):
        for copy in pair_loads(index):
            copy.start()

    def score_block(low, value, grad, column):
        return low.astype(f32) * (dot(value, grad, NT) - column)

    def body(index, carry):
        @pl.when(index + 1 < count)
        def _():
            slot_copy(index + 1).start()

        lanes = pair_lanes(index)
        slot = lax.rem(index, 2)
        for copy in pair_loads(index):
            copy.wait()
        key_block, value_block, query_block, grad_block = v_k[:, lanes], v_v[:, lanes], v_q[:, lanes], v_grad[:, lanes]
        inv_rows = inverse[pl.ds(first + index, 1)][0]
        inv_columns = jnp.concatenate([inv_rows, jnp.zeros((8 - per, inv_rows.shape[1]), f32)], axis=0).T
        scaled = grad_block.astype(f32) * sum(inv_columns[:, i : i + 1] * masks[i] for i in range(per))
        scaled = scaled.astype(bf16)
        product = scaled.astype(f32) * v_mix[:, lanes]
        columns = [jnp.sum(product * masks[i], axis=1, keepdims=True) for i in range(per)]
        wide_columns = sum(c * (lax.broadcasted_iota(jnp.int32, (1, 8), 1) == i).astype(f32) for i, c in enumerate(columns))
        column_rows = wide_columns.T
        slot_copy(index).wait()
        grads = [0.0, 0.0, 0.0]
        for i in range(per):
            column = column_rows[i : i + 1, :]
            grad = scaled * masks[i].astype(bf16)
            if fold:
                edge = grad.shape[0] // 2
                low, high = slice(0, edge), slice(edge, 2 * edge)
                cuts = ((low, low), (low, high), (high, high))
                probs_at = [slots[slot, i, k, q] for k, q in cuts]
                scores = [score_block(p, value_block[k], grad[q], column[:, q]) for p, (k, q) in zip(probs_at, cuts)]
                v_dist[index * per + i] = fold_diagonals(jnp.concatenate([scores[0] + scores[2], scores[1]], axis=1))
                lows = [x.astype(bf16) for x in scores]
                dq = [dot(lows[0], key_block[low], TN), dot(lows[1], key_block[low], TN) + dot(lows[2], key_block[high], TN)]
                dk = [dot(lows[0], query_block[low], NN) + dot(lows[1], query_block[high], NN), dot(lows[2], query_block[high], NN)]
                dv = [dot(probs_at[0], scaled[low], NN) + dot(probs_at[1], scaled[high], NN), dot(probs_at[2], scaled[high], NN)]
                terms_of = [jnp.concatenate(x, axis=0) for x in (dq, dk, dv)]
            else:
                probs_all = slots[slot, i]
                score_low = score_block(probs_all, value_block, grad, column).astype(bf16)
                terms_of = [dot(score_low, key_block, TN), dot(score_low, query_block, NN), dot(probs_all, scaled, NN)]
            grads = [g + x * masks[i] for g, x in zip(grads, terms_of)]
        v_dq[:, lanes] = grads[0].astype(bf16)
        v_dk[:, lanes] = grads[1].astype(bf16)
        v_dv[:, lanes] = grads[2].astype(bf16)
        for copy in pair_stores(index):
            copy.start()
        return carry

    lax.fori_loop(0, count, body, 0)
    if fold:
        dist_copy = pltpu.make_async_copy(v_dist, o_dist.at[pl.ds(first * per, count * per)], sems.at[0, 8])
        dist_copy.start()
        dist_copy.wait()
    for index in range(count):
        for copy in pair_stores(index):
            copy.wait()


def attend_back(order, head_size, fold, first, count, inverse, probs, exact_mix, grad_mixed, queries, keys, values, earlier=()):
    t, d = queries.shape
    e = keys.shape[0]
    per = LANES // head_size
    td, ed = (t, count * LANES), (e, count * LANES)
    out_shape = [shaped((t, d), bf16), shaped((e, d), bf16), shaped((e, d), bf16)]
    if fold:
        out_shape.append(shaped((d // head_size, 8, t), f32))
    scratch = [pltpu.VMEM(td, f32)] + [pltpu.VMEM(s, bf16) for s in (td, td, ed, ed, td, ed, ed)]
    scratch += [pltpu.VMEM((2, per, e, t), bf16), pltpu.SemaphoreType.DMA((count, 9)), pltpu.SemaphoreType.DMA((2,))]
    if fold:
        scratch.append(pltpu.VMEM((count * per, 8, t), f32))
    return order.call(
        partial(attend_back_kernel, head_size, fold, first, count, len(earlier)),
        out_shape=out_shape,
        in_specs=[VM] + [HBM] * (6 + len(earlier)),
        out_specs=[HBM] * len(out_shape),
        input_output_aliases={7 + i: i for i in range(len(earlier))},
        scratch_shapes=scratch,
        vmem=32,
        name="attend_back",
    )(inverse, probs, exact_mix, grad_mixed, queries, keys, values, *earlier)


def terms_kernel(count, place, *refs):
    lefts, rights, out = refs[:count], refs[count : 2 * count], refs[2 * count]
    v_lefts, v_rights, sent, sems = refs[2 * count + 1 : 3 * count + 1], refs[3 * count + 1 : 4 * count + 1], refs[-2], refs[-1]
    rows = out.shape[2]
    moves = Moves(sems)
    lanes = half_lanes(1 - place[0], 2 * rows)
    got = [(moves.load(lefts[u], v_lefts[u]), moves.load(rights[u].at[:, lanes], v_rights[u])) for u in range(count)]
    for u in range(count):
        here = pl.ds(u * rows, rows)
        for copy in got[u]:
            copy.wait()
        for b in range(2):
            sent[b, here, :] = dot(v_lefts[u][:, b * rows : (b + 1) * rows], v_rights[u][...], TN)
            moves.store(sent.at[b, here], out.at[b, here])
    moves.finish()


def terms(order, place, lefts, rights):
    count = len(lefts)
    d = lefts[0].shape[1]
    out = (2, count * (d // 2), d // 2)
    return order.call(
        partial(terms_kernel, count),
        out_shape=shaped(out, f32),
        in_specs=[SM] + [HBM] * (2 * count),
        out_specs=HBM,
        scratch_shapes=[pltpu.VMEM(x.shape, bf16) for x in lefts]
        + [pltpu.VMEM((x.shape[0], d // 2), bf16) for x in rights]
        + [pltpu.VMEM(out, f32), pltpu.SemaphoreType.DMA((4 * count,))],
        vmem=24,
        name="terms",
    )(place, *lefts, *rights)


def terms_kept_kernel(count, axes, place, *refs):
    lefts, rights = refs[:count], refs[count : 2 * count]
    sent, o_send, o_keep = refs[2 * count : 2 * count + 3]
    v_lefts, v_rights = refs[2 * count + 3 : 3 * count + 3], refs[3 * count + 3 : 4 * count + 3]
    v_sent, full, sems = refs[4 * count + 3 :]
    rows = sent.shape[2]
    moves = Moves(sems)
    lanes = half_lanes(place[0], 2 * rows)
    got = []
    for u in range(count):
        here = pl.ds(u * rows, rows)
        got.append(
            (
                moves.load(lefts[u], v_lefts[u]),
                moves.load(rights[u].at[:, lanes], v_rights[u]),
                moves.load(sent.at[:, here], v_sent.at[:, here]),
            )
        )
    for u in range(count):
        here = slice(u * rows, (u + 1) * rows)
        for copy in got[u]:
            copy.wait()
        for b in range(2):
            full[b, here, :] = v_sent[b, here, :] + dot(v_lefts[u][:, b * rows : (b + 1) * rows], v_rights[u][...], TN)
    cut_first(axes, place, full, o_send, o_keep)


def terms_kept(order, axes, place, lefts, rights, sent):
    count = len(lefts)
    d = lefts[0].shape[1]
    return order.call(
        partial(terms_kept_kernel, count, axes),
        out_shape=[shaped(sent.shape[1:], f32)] * 2,
        in_specs=[SM] + [HBM] * (2 * count) + [ANY],
        out_specs=[VM] * 2,
        scratch_shapes=[pltpu.VMEM(x.shape, bf16) for x in lefts]
        + [pltpu.VMEM((x.shape[0], d // 2), bf16) for x in rights]
        + [pltpu.VMEM(sent.shape, f32), pltpu.VMEM(sent.shape, f32), pltpu.SemaphoreType.DMA((3 * count,))],
        vmem=30,
        name="terms_kept",
    )(place, *lefts, *rights, sent)


def cross_close_kernel(
    rows, grad_two, stream1, dq, cq, wo, o_grad, o_low, o_mixed, o_gain,
    v_two, v_stream, v_dq, v_cq, v_wo, grad, low, mixed, sems,
):
    moves = Moves(sems)
    sources = (dq, cq, stream1, grad_two, wo)
    got = [moves.load(s, t) for s, t in zip(sources, (v_dq, v_cq, v_stream, v_two, v_wo))]
    for copy in got[:2]:
        copy.wait()
    back = dot(v_dq[...], v_cq[...], NT)
    for copy in got[2:4]:
        copy.wait()
    pulled, gain_grad = norm_pull(back, v_stream[...], rows[1:2, :])
    o_gain[...] = gain_grad
    grad[...] = v_two[...] + pulled
    moves.store(grad, o_grad)
    low[...] = grad[...].astype(bf16)
    moves.store(low, o_low)
    got[4].wait()
    mixed[...] = dot(low[...], v_wo[...], NT).astype(bf16)
    moves.store(mixed, o_mixed)
    moves.finish()


def cross_close(order, rows, grad_two, stream1, dq, cq, wo):
    t, d = dq.shape
    td, dd = (t, d), (d, d)
    return order.call(
        cross_close_kernel,
        out_shape=[shaped(td, f32), shaped(td, bf16), shaped(td, bf16), shaped((1, d), f32)],
        in_specs=[VM] + [HBM] * 5,
        out_specs=[HBM] * 3 + [VM],
        scratch_shapes=[pltpu.VMEM(td, f32), pltpu.VMEM(td, f32)]
        + [pltpu.VMEM(s, bf16) for s in (td, dd, dd)]
        + [pltpu.VMEM(td, f32), pltpu.VMEM(td, bf16), pltpu.VMEM(td, bf16)]
        + [pltpu.SemaphoreType.DMA((8,))],
        vmem=20,
        name="cross_close",
    )(rows, grad_two, stream1, dq, cq, wo)


def enc_close_kernel(dk, dv, ck, cv, out, v_dk, v_dv, v_ck, v_cv, total, sems):
    moves = Moves(sems)
    got = [moves.load(s, t) for s, t in ((dk, v_dk), (ck, v_ck), (dv, v_dv), (cv, v_cv))]
    for copy in got:
        copy.wait()
    rows = out.shape[0] // 2
    for i in range(2):
        here = pl.ds(i * rows, rows)
        total[here, :] = dot(v_dk[here, :], v_ck[...], NT) + dot(v_dv[here, :], v_cv[...], NT)
        moves.store(total.at[here], out.at[here])
    moves.finish()


def enc_close(order, dk, dv, ck, cv):
    e, d = dk.shape
    return order.call(
        enc_close_kernel,
        out_shape=shaped((e, d), f32),
        in_specs=[HBM] * 4,
        out_specs=HBM,
        scratch_shapes=[pltpu.VMEM((e, d), bf16)] * 2
        + [pltpu.VMEM((d, d), bf16)] * 2
        + [pltpu.VMEM((e, d), f32), pltpu.SemaphoreType.DMA((6,))],
        vmem=20,
        name="enc_close",
    )(dk, dv, ck, cv)


def self_close_kernel(
    table_shape, flag, rows, gain_b, gain_c, grad_one, dec, dq, dk, dv, dist, wq, wk, wv, o_grad, o_small,
    v_one, v_dec, v_dq, v_dk, v_dv, v_dist, v_wq, v_wk, v_wv, grad_zero, sems,
):
    t, d = dq.shape
    heads = dist.shape[0]
    num_buckets = table_shape[0]
    moves = Moves(sems)
    sources = (dq, wq, dk, wk, dv, wv, dec, grad_one, dist)
    targets = (v_dq, v_wq, v_dk, v_wk, v_dv, v_wv, v_dec, v_one, v_dist)
    got = [moves.load(s, t_) for s, t_ in zip(sources, targets)]
    dir_row = jnp.where(flag[0] == 0, rows[3:4, :], rows[4:5, :])
    back = None
    for i, (grad, weight) in enumerate(((v_dq, v_wq), (v_dk, v_wk), (v_dv, v_wv))):
        got[2 * i].wait()
        got[2 * i + 1].wait()
        term = dot(grad[...], weight[...], NT)
        back = term if back is None else back + term
    got[6].wait()
    got[7].wait()
    pulled, gain_grad = norm_pull(back, v_dec[...].astype(f32) + dir_row, rows[0:1, :])
    grad_zero[...] = v_one[...] + pulled
    moves.store(grad_zero, o_grad)
    row_sum = jnp.sum(grad_zero[...], axis=0, keepdims=True)
    picked = (flag[0] == 0).astype(f32)
    o_small[...] = jnp.zeros(o_small.shape, f32)
    o_small[0:1, :] = gain_grad
    o_small[1:2, :] = gain_b[...]
    o_small[2:3, :] = gain_c[...]
    o_small[3:4, :] = row_sum * picked
    o_small[4:5, :] = row_sum * (1.0 - picked)
    pick = lax.broadcasted_iota(jnp.int32, (num_buckets, t), 0).astype(f32) == rows[5:6, :t]
    got[8].wait()
    per_head = [jnp.sum(v_dist[h], axis=0, keepdims=True) for h in range(heads)]
    per_head += [jnp.zeros((1, t), f32)] * (-heads % 8)
    table = lax.dot_general(
        jnp.where(pick, 1.0, 0.0).astype(f32),
        jnp.concatenate(per_head, axis=0),
        NT,
        precision=lax.Precision.HIGHEST,
        preferred_element_type=f32,
    )
    o_small[8:, 0 : table.shape[1]] = table
    moves.finish()


def self_close(order, table_shape, flag, rows, gain_b, gain_c, grad_one, dec, dq, dk, dv, dist, wq, wk, wv):
    t, d = dq.shape
    td, dd = (t, d), (d, d)
    return order.call(
        partial(self_close_kernel, table_shape),
        out_shape=[shaped(td, f32), shaped((8 + table_shape[0], d), f32)],
        in_specs=[SM, VM, VM, VM] + [HBM] * 9,
        out_specs=[HBM, VM],
        scratch_shapes=[pltpu.VMEM(td, f32)]
        + [pltpu.VMEM(td, bf16)] * 4
        + [pltpu.VMEM(dist.shape, f32)]
        + [pltpu.VMEM(dd, bf16)] * 3
        + [pltpu.VMEM(td, f32), pltpu.SemaphoreType.DMA((10,))],
        vmem=24,
        name="self_close",
    )(flag, rows, gain_b, gain_c, grad_one, dec, dq, dk, dv, dist, wq, wk, wv)


class Links:
    def __init__(self, dp, rep):
        self.dp, self.rep = dp, rep
        self.lines = dp // 4

    def send(self, value, target):
        pairs = []
        for i in range(self.dp):
            for r in range(self.rep):
                line, side, core, to_rep = target(i // 4, i // 2 % 2, i % 2, r)
                pairs.append((i * self.rep + r, ((line * 2 + side) * 2 + core) * self.rep + to_rep))
        return lax.ppermute(value, ("dp", "rep"), pairs)

    def core(self, value):
        return self.send(value, lambda line, side, core, r: (line, side, core ^ 1, r))

    def line(self, value, flip):
        return self.send(value, lambda line, side, core, r: (line ^ flip, side, core, r))

    def swap(self, value, axes):
        def target(line, side, core, r):
            axis = axes[core]
            return line ^ (axis == "z"), side ^ (axis == "x"), core, r ^ (axis == "y")

        return self.send(value, target)

    def line_flips(self, first):
        flips = []
        while first < self.lines:
            flips.append(first)
            first *= 2
        return flips


def mebibytes(*arrays):
    return 2 + sum(-(-math.prod(a.shape) * 4 // 2**20) for a in arrays)


def add(order, a, b):
    def kernel(left, right, out):
        out[...] = left[...] + right[...]

    return order.call(
        kernel,
        in_specs=[VM, VM],
        out_specs=VM,
        out_shape=shaped(a.shape, f32),
        vmem=mebibytes(a, b, a),
        name="add",
    )(a, b)


def split_add(order, axes, place, keep, got):
    keep, got = (x.reshape((2, -1, x.shape[-1])) for x in (keep, got))

    def kernel(at, left, right, o_send, o_mine):
        mine = bit_of(at, axes)
        o_send[...] = left[1 - mine] + right[1 - mine]
        o_mine[...] = left[mine] + right[mine]

    return order.call(
        kernel,
        in_specs=[SM, VM, VM],
        out_specs=[VM, VM],
        out_shape=[shaped(keep.shape[1:], f32)] * 2,
        vmem=mebibytes(keep, got, keep),
        name="split_add",
    )(place, keep, got)


def join(order, axes, place, mine, far):
    def kernel(at, left, right, out):
        bit = bit_of(at, axes)
        out[bit] = left[...]
        out[1 - bit] = right[...]

    out = order.call(
        kernel,
        in_specs=[SM, VM, VM],
        out_specs=VM,
        out_shape=shaped((2,) + mine.shape, f32),
        vmem=mebibytes(mine, far, mine, far),
        name="join",
    )(place, mine, far)
    return out.reshape((-1, mine.shape[-1]))


def sum_bundle(order, links, place, ways, send, keep):
    steps = list(zip(*ways))
    back = list(zip(*([axis for axis in reversed(way) if axis != "y"] for way in ways)))
    got = links.swap(send, steps[0])
    yield
    for axes in steps[1:]:
        send, keep = split_add(order, axes, place, keep, got)
        got = links.swap(send, axes)
        yield
    mine = add(order, keep, got)
    for flip in links.line_flips(2):
        got = links.line(mine, flip)
        yield
        mine = add(order, mine, got)
    for axes in back:
        got = links.swap(mine, axes)
        yield
        mine = join(order, axes, place, mine, got)
    got = links.core(mine)
    yield
    return mine, got


def place_kernel(segments, aliased, place, mine, other, *refs):
    outs, sems = refs[aliased:-1], refs[-1]
    copies = []
    for i, (piece, core) in enumerate(((mine, place[0]), (other, 1 - place[0]))):
        for j, (first, count, out, row, base, step) in enumerate(segments):
            lanes = pl.ds(pl.multiple_of(base + core * step, LANES), piece.shape[1])
            copies.append(
                pltpu.make_async_copy(piece.at[pl.ds(first, count)], outs[out].at[pl.ds(row, count), lanes], sems.at[i, j])
            )
    for copy in copies:
        copy.start()
    for copy in copies:
        copy.wait()


def place_pieces(order, place, pieces, segments, out_shapes, aliased=()):
    return order.call(
        partial(place_kernel, segments, len(aliased)),
        in_specs=[SM, VM, VM] + [HBM] * len(aliased),
        out_specs=[HBM] * len(out_shapes),
        out_shape=out_shapes,
        input_output_aliases={3 + i: i for i in range(len(aliased))},
        scratch_shapes=[pltpu.SemaphoreType.DMA((2, len(segments)))],
        vmem=mebibytes(*pieces[:2]),
        name="place",
    )(place, *pieces, *aliased)


def sum_small(order, links, small):
    for axes in ("yy", "xx", "zz"):
        got = links.swap(small, axes)
        yield
        small = add(order, small, got)
    for flip in links.line_flips(2):
        got = links.line(small, flip)
        yield
        small = add(order, small, got)
    got = links.core(small)
    yield
    return add(order, small, got)


class Live:
    def __init__(self, steps):
        self.steps, self.result = steps, None
        self.step()

    def step(self):
        if self.result is None:
            try:
                next(self.steps)
            except StopIteration as end:
                self.result = end.value

    def finish(self):
        while self.result is None:
            self.step()
        return self.result


PLAN = (
    "fwd", "feed0", "feed1", "kept0", "result", "kept1", "close", "attb0", "F0", "attb1", "cterm0", "F1", "enc", "F0",
    "ckept0", "cclose", "F1", "F0", "atta0", "oterm0", "C0", "F1", "oterm1", "okept0", "F0", "okept1", "C0", "O0",
    "F0", "F1", "C0", "O1", "F1", "O0", "F0", "C0", "F0p", "O0", "O1", "sclose", "C0", "S", "O0", "F1", "O1", "O0",
    "F1p", "O1", "C0", "S", "O1", "S", "C0p", "S", "O0", "S", "O0p", "O1", "O1p",
)
FEED_CUTS = (2, 2)
FEED_WAYS = (("yxz", "xyz"), ("yxz", "xyz"))
CROSS_WAYS = (("yxz", "xyz"),)
OWN_WAYS = (("yxz", "xyz"), ("yxz", "xyz"))
ATTEND = (2, 1)


def local(
    dp, rep,
    dec_input, enc_states, out_cotangent, dec_lengths, group_ids, direction_flags, rel_buckets, step_index,
    self_gain, self_query, self_key, self_value, self_output, bucket_bias_table,
    cross_gain, cross_query, cross_key, cross_value, cross_output, feed_gain, feed_inner, feed_outer, dir_table,
):
    dec, enc, cot = dec_input[0], enc_states[0], out_cotangent[0]
    num_buckets, num_heads = bucket_bias_table.shape
    d = dec.shape[1]
    half = d // 2
    head_size = d // num_heads
    pairs = d // LANES
    links = Links(dp, rep)
    dp_index, rep_index = lax.axis_index("dp"), lax.axis_index("rep")
    place = jnp.stack([dp_index % 2, rep_index, (dp_index // 4) % 2, (dp_index // 2) % 2]).astype(jnp.int32)
    phase = full_turn * step_index.astype(f32) / PERIOD
    weight = 1.0 + 0.5 * jnp.cos(phase + full_turn * group_ids.astype(f32) / 3.0)
    length, flag = dec_lengths, direction_flags
    order = Order()
    env = {}
    live = {}
    block = feed_inner.shape[1] // 2
    starts = [sum(FEED_CUTS[:i]) for i in range(len(FEED_CUTS))]
    cuts = tuple((a * half, n * half) for a, n in zip(starts, FEED_CUTS))
    actives, pulls, sents = {}, {}, {}
    outer_shape = shaped((feed_outer.shape[0] // rep, d), f32)
    inner_shape = shaped((d // rep, feed_inner.shape[1]), f32)
    feed_grads = []
    done = {}

    def run_forward():
        names = (
            "input_a", "q", "k", "v", "mixed_a", "stream1", "input_b", "xq", "ek", "ev", "mixed_b", "stream2", "input_c",
            "probs_a", "probs_b", "exact_a", "exact_b", "rows", "inv_a", "inv_b",
        )
        smalls = (self_gain, cross_gain, feed_gain, dir_table, rel_buckets, bucket_bias_table.T)
        weights = (self_query, self_key, self_value, self_output, cross_query, cross_key, cross_value, cross_output)
        env.update(zip(names, forward(order, head_size, num_buckets, flag, smalls, dec, enc, weights)))

    def run_feed(p):
        actives[p], pulls[p], sent = feed(order, *cuts[p], place, weight, length, cot, env["input_c"], feed_inner, feed_outer)
        sents[p] = links.core(sent)

    def run_kept(p):
        first = [way[0] for way in FEED_WAYS[p]]
        send, keep = feed_kept(order, first, place, weight, length, cot, env["input_c"], actives[p], pulls[p], sents[p])
        live[f"F{p}"] = Live(sum_bundle(order, links, place, FEED_WAYS[p], send, keep))

    def run_close():
        pulled = [pulls[i] for i in range(len(cuts))]
        outs = close(order, cuts, weight, length, env["rows"], cot, env["stream2"], pulled, feed_inner, cross_output)
        env.update(zip(("grad_two", "low_two", "grad_mixed_b", "gain_c_grad"), outs))

    def run_result():
        active = [actives[i] for i in range(len(cuts))]
        env["block_output"] = block_result(order, cuts, length, env["stream2"], active, feed_outer)

    def run_attend(i, groups, fold, name, *args):
        count = pairs // groups
        env[name] = attend_back(order, head_size, fold, i * count, count, *(env[a] for a in args), earlier=env.get(name, ()))

    def run_cross_close():
        outs = cross_close(
            order, env["rows"], env["grad_two"], env["stream1"], env["back_b"][0], cross_query, self_output
        )
        env.update(zip(("grad_one", "low_one", "grad_mixed_a", "gain_b_grad"), outs))

    def run_enc_close():
        env["enc_grad"] = enc_close(order, *env["back_b"][1:], cross_key, cross_value)

    def run_self_close():
        outs = self_close(
            order, bucket_bias_table.shape, flag, env["rows"], env["gain_b_grad"], env["gain_c_grad"], env["grad_one"], dec,
            *env["back_a"], self_query, self_key, self_value,
        )
        env["input_grad"], small = outs
        live["S"] = Live(sum_small(order, links, small))

    def operands(own):
        if own:
            dq, dk, dv, _ = env["back_a"]
            return (env["mixed_a"], env["input_a"], env["input_a"], env["input_a"]), (env["low_one"], dq, dk, dv)
        dq, dk, dv = env["back_b"]
        return (env["mixed_b"], env["input_b"], enc, enc), (env["low_two"], dq, dk, dv)

    def piece(own, i):
        count = 4 // len(OWN_WAYS if own else CROSS_WAYS)
        return [x[i * count : (i + 1) * count] for x in operands(own)]

    def run_terms(own, i):
        sents[own, i] = links.core(terms(order, place, *piece(own, i)))

    def run_terms_kept(own, i):
        ways = (OWN_WAYS if own else CROSS_WAYS)[i]
        send, keep = terms_kept(order, [way[0] for way in ways], place, *piece(own, i), sents[own, i])
        live[f"{'O' if own else 'C'}{i}"] = Live(sum_bundle(order, links, place, ways, send, keep))

    def run_place(name):
        pieces = live[name].finish()
        if name[0] == "F":
            offset, split = cuts[int(name[1:])]
            segments = [(0, split, 0, offset, 0, half)]
            segments += [(split + i * half, half, 1, 0, offset + i * half, block) for i in range(split // half)]
            feed_grads[:] = place_pieces(order, place, pieces, segments, [outer_shape, inner_shape], feed_grads)
        else:
            count = 4 // len(OWN_WAYS if name[0] == "O" else CROSS_WAYS)
            segments = [(j * half, half, j, 0, 0, half) for j in range(count)]
            done[name] = place_pieces(order, place, pieces, segments, [shaped((half, d), f32)] * count)

    for name in PLAN:
        head = name.rstrip("0123456789p")
        index = int(name[len(head)]) if name[-1].isdigit() else None
        if name == "fwd":
            run_forward()
        elif head == "feed":
            run_feed(index)
        elif head == "kept":
            run_kept(index)
        elif name == "close":
            run_close()
        elif name == "result":
            run_result()
        elif name == "enc":
            run_enc_close()
        elif head == "attb":
            run_attend(index, ATTEND[0], False, "back_b", "inv_b", "probs_b", "exact_b", "grad_mixed_b", "xq", "ek", "ev")
        elif head == "atta":
            run_attend(index, ATTEND[1], True, "back_a", "inv_a", "probs_a", "exact_a", "grad_mixed_a", "q", "k", "v")
        elif name == "cclose":
            run_cross_close()
        elif name == "sclose":
            run_self_close()
        elif head in ("oterm", "cterm"):
            run_terms(head == "oterm", index)
        elif head in ("okept", "ckept"):
            run_terms_kept(head == "okept", index)
        elif name.endswith("p"):
            run_place(name[:-1])
        else:
            live[name].step()

    outer, inner = feed_grads
    small = live["S"].finish()
    cross = [x for i in range(len(CROSS_WAYS)) for x in done[f"C{i}"]]
    own = [x for i in range(len(OWN_WAYS)) for x in done[f"O{i}"]]
    small_rows = lambda i: lax.dynamic_slice_in_dim(small[i], rep_index * half, half)
    table_rows = num_buckets // rep
    table = lax.dynamic_slice(small, (8 + rep_index * table_rows, 0), (table_rows, num_heads))
    dir_grad = lax.dynamic_slice_in_dim(small, 3 + rep_index, 1)
    return (
        env["block_output"][None],
        env["input_grad"][None],
        env["enc_grad"][None],
        small_rows(0),
        own[1],
        own[2],
        own[3],
        own[0],
        table,
        small_rows(1),
        cross[1],
        cross[2],
        cross[3],
        cross[0],
        small_rows(2),
        inner,
        outer,
        dir_grad,
    )


def solution(mesh):
    pair = P(("dp", "rep"), None, None)
    each = P(("dp", "rep"))
    rows = P("rep", None)
    vector = P("rep")
    return jax.shard_map(
        partial(local, mesh.shape["dp"], mesh.shape["rep"]),
        mesh=mesh,
        in_specs=(pair, pair, pair, each, each, each) + (P(),) * 17,
        out_specs=(
            pair, pair, pair, vector, rows, rows, rows, rows, rows, vector, rows, rows, rows, rows, vector, rows, rows, rows,
        ),
        check_vma=False,
    )
```
